32 devices in a mesh: band: 4 (over y, x), domain: 8 (over z, core).
Axes of the slice: x: 2, y: 2, z: 4, core: 2. Of those that a mesh axis runs over, the one named last changes fastest.
Arguments:
- functions: bfloat16 [512, 24576], P(('band', 'domain')), may hold values from -6 to 6
- pattern: int32 [4, 4], replicated, may hold values from 0 to 3, as said below
Outputs:
- corrected: bfloat16 [512, 24576], P(('band', 'domain'))
The draws below stay inside these ranges and needn't reach their ends.
Inputs may be any that keep to these rules, and one draw needn't show every extreme that they name: Row b of pattern holds 4 different block numbers, and its first entry is b itself. The pattern is symmetric: j stands in row b exactly when b stands in row j.
All inputs are finite; a program needn't handle non-finite values.
Results may differ from the reference program's by a relative error of at most 0.0037.
Values may be sent and summed in bfloat16 or wider, within the bound.
No kernel may reach another device: no remote copies, remote signals or barrier semaphores. Data moves between devices by JAX's collectives and lax.ppermute only.
A program may use at most 192 MiB of HBM per device.

```python
import jax
import jax.numpy as jnp
from jax import lax

NC = 24576
BLOCK = 128
NF = 512
NNZ = 4


def draw_pattern(key, part):
    count = NF // BLOCK
    half_way = count // 2
    picks = (NNZ - 2) // 2
    chosen = jax.random.permutation(jax.random.fold_in(key, 1), half_way - 1).astype(jnp.int32)[:picks] + 1
    offsets = jnp.concatenate([jnp.zeros((1,), jnp.int32), chosen, count - chosen, jnp.full((1,), half_way, jnp.int32)])
    relabel = jax.random.permutation(jax.random.fold_in(key, 2), count).astype(jnp.int32)
    inverse = jnp.zeros((count,), jnp.int32).at[relabel].set(jnp.arange(count, dtype=jnp.int32))
    places = (inverse[:, None] + offsets[None, :]) % count
    return jnp.take(relabel, places.reshape(-1), axis=0).reshape(count, NNZ).astype(jnp.int32)


def shard_levels(rng, shape, shards, low, top_value):
    def one(position, shards_of):
        draws = jax.random.uniform(jax.random.fold_in(jax.random.fold_in(rng, 6), position), (shards_of,), jnp.float32, low / len(shards), top_value / len(shards))
        return jnp.repeat(jnp.exp(draws), shape[position] // shards_of).reshape((-1,) + (1,) * (len(shape) - position - 1))

    gain = one(*shards[0])
    for cut in shards[1:]:
        gain = gain * one(*cut)
    return gain


def bell_draw(own_key, extent, spread, most, cuts=(), held_as=jnp.bfloat16):
    factor_of = shard_levels(own_key, extent, cuts, -0.22, 0.18) if cuts else 1.0
    result = jax.random.normal(own_key, extent, jnp.float32) * spread * factor_of
    return jnp.minimum(jnp.maximum(result, -most), most).astype(held_as)


def setup_inputs(seed: int = 0) -> dict:
    streams_of = jax.random.split(jax.random.key(seed), 3)
    functions = bell_draw(streams_of[0], (NF, NC), 1.3, 6.0, ((0, 32),))
    pattern = draw_pattern(jax.random.fold_in(streams_of[2], 71), 0)
    return dict(functions=functions, pattern=pattern)


def reference(functions, pattern):
    count = NF // BLOCK
    phi = functions.astype(jnp.float32).reshape(count, BLOCK, NC)
    eye = jnp.eye(BLOCK, dtype=jnp.float32)

    def intersection_row(brow):
        cols = jnp.take(phi, pattern[brow], axis=0)
        mine = lax.dynamic_index_in_dim(phi, brow, 0, keepdims=False)
        inner = jnp.einsum("ic,kjc->kij", mine, cols, precision=lax.Precision.HIGHEST) * (1.0 / NC)
        diag = (pattern[brow] == brow).astype(jnp.float32)
        return (inner - diag[:, None, None] * eye).astype(jnp.bfloat16)

    rows = jnp.arange(count, dtype=jnp.int32)
    excess = lax.map(intersection_row, rows)

    def apply_row(source, brow):
        cols = jnp.take(source, pattern[brow], axis=0)
        block = lax.dynamic_index_in_dim(excess, brow, 0, keepdims=False).astype(jnp.float32)
        return jnp.einsum("kij,kjc->ic", block, cols, precision=lax.Precision.HIGHEST)

    first = lax.map(lambda brow: apply_row(phi, brow), rows)
    first_half = first.astype(jnp.bfloat16).astype(jnp.float32)
    second = lax.map(lambda brow: apply_row(first_half, brow), rows)
    corrected = phi - 0.5 * first + 0.375 * second
    return corrected.astype(jnp.bfloat16).reshape(NF, NC)
```

```python
import functools

import jax
import jax.numpy as jnp
from jax import lax
from jax.experimental import pallas as pl
from jax.experimental.pallas import tpu as pltpu
from jax.sharding import PartitionSpec as P

NC = 24576
BLOCK = 128
BOTH = ("band", "domain")


def vmem_call(body, outs, scratch=(), flops=0, moved=0):
    return pl.pallas_call(
        body,
        out_shape=outs,
        scratch_shapes=list(scratch),
        cost_estimate=pl.CostEstimate(flops=flops, bytes_accessed=moved, transcendentals=0),
        compiler_params=pltpu.CompilerParams(vmem_limit_bytes=48 * 1024 * 1024),
    )


def swap(value, axis, mask):
    count = lax.axis_size(axis)
    return lax.ppermute(value, axis, [(i, i ^ mask) for i in range(count)])


def upper_blocks(nblocks):
    return [(i, j) for i in range(nblocks) for j in range(i, nblocks)]


def gram_halves(x, share):
    rows, width = x.shape
    nblocks = rows // BLOCK
    pairs = upper_blocks(nblocks)
    half = len(pairs) * BLOCK // 2
    tile = 2 * BLOCK

    def body(core_ref, x_ref, keep_ref, give_ref):
        core = core_ref[0]
        eye = (
            lax.broadcasted_iota(jnp.int32, (BLOCK, BLOCK), 0) == lax.broadcasted_iota(jnp.int32, (BLOCK, BLOCK), 1)
        ).astype(jnp.float32) * share
        for a in range(rows // tile):
            for b in range(a, rows // tile):
                got = lax.dot_general(
                    x_ref[a * tile:(a + 1) * tile, :],
                    x_ref[b * tile:(b + 1) * tile, :],
                    (((1,), (1,)), ((), ())),
                    preferred_element_type=jnp.float32,
                )
                for i in range(2):
                    for j in range(2):
                        pair = (2 * a + i, 2 * b + j)
                        if pair not in pairs:
                            continue
                        block = got[i * BLOCK:(i + 1) * BLOCK, j * BLOCK:(j + 1) * BLOCK]
                        if pair[0] == pair[1]:
                            block = block - eye
                        start = pairs.index(pair) * BLOCK
                        side, at = start // half, start % half

                        @pl.when(core == side)
                        def _():
                            keep_ref[at:at + BLOCK, :] = block

                        @pl.when(core != side)
                        def _():
                            give_ref[at:at + BLOCK, :] = block

    stacked = jax.ShapeDtypeStruct((half, BLOCK), jnp.float32)
    return pl.pallas_call(
        body,
        out_shape=(stacked, stacked),
        in_specs=[pl.BlockSpec(memory_space=pltpu.SMEM), pl.BlockSpec(memory_space=pltpu.VMEM)],
        compiler_params=pltpu.CompilerParams(vmem_limit_bytes=48 * 1024 * 1024),
    )


def band_pieces(half, bands):
    piece = half // bands

    def body(band_ref, keep_ref, got_ref, *piece_refs):
        band = band_ref[0]
        for m in range(bands):
            at = pl.ds(pl.multiple_of((band ^ m) * piece, piece), piece)
            piece_refs[m][...] = keep_ref[at, :] + got_ref[at, :]

    return pl.pallas_call(
        body,
        out_shape=tuple(jax.ShapeDtypeStruct((piece, BLOCK), jnp.float32) for _ in range(bands)),
        in_specs=[pl.BlockSpec(memory_space=pltpu.SMEM)] + [pl.BlockSpec(memory_space=pltpu.VMEM)] * 2,
    )


def correct(x, pieces, bands):
    rows, width = x.shape
    nblocks = rows // BLOCK
    pairs = upper_blocks(nblocks)
    half = len(pairs) * BLOCK // 2
    piece = half // bands

    def body(place_ref, x_ref, *refs):
        piece_refs, out_ref, packed, excess = refs[:-3], refs[-3], refs[-2], refs[-1]
        band, core = place_ref[0], place_ref[1]
        for m in range(bands):
            for c in range(2):
                start = (core ^ c) * half + (band ^ m) * piece
                packed[pl.ds(pl.multiple_of(start, 16), piece), :] = piece_refs[c * bands + m][...]
        for p, (i, j) in enumerate(pairs):
            block = packed[p * BLOCK:(p + 1) * BLOCK, :]
            excess[i * BLOCK:(i + 1) * BLOCK, j * BLOCK:(j + 1) * BLOCK] = block
            if i != j:
                excess[j * BLOCK:(j + 1) * BLOCK, i * BLOCK:(i + 1) * BLOCK] = block.T
        first = jnp.dot(excess[...], x_ref[...], preferred_element_type=jnp.float32)
        second = jnp.dot(excess[...], first.astype(jnp.bfloat16), preferred_element_type=jnp.float32)
        out = x_ref[...].astype(jnp.float32) - 0.5 * first + 0.375 * second
        out_ref[...] = out.astype(jnp.bfloat16)

    return pl.pallas_call(
        body,
        out_shape=jax.ShapeDtypeStruct(x.shape, jnp.bfloat16),
        in_specs=[pl.BlockSpec(memory_space=pltpu.SMEM)] + [pl.BlockSpec(memory_space=pltpu.VMEM)] * (1 + 2 * bands),
        scratch_shapes=[
            pltpu.VMEM((2 * half, BLOCK), jnp.bfloat16),
            pltpu.VMEM((rows, rows), jnp.bfloat16),
        ],
        compiler_params=pltpu.CompilerParams(vmem_limit_bytes=48 * 1024 * 1024),
    )


def full_rows(functions, pattern):
    bands, domains = lax.axis_size("band"), lax.axis_size("domain")
    devices = bands * domains
    fdev, ncoef = functions.shape
    width = ncoef // devices
    x = lax.all_to_all(functions, BOTH, split_axis=1, concat_axis=0, tiled=True)
    band = lax.axis_index("band").astype(jnp.int32)
    core = lax.rem(lax.axis_index("domain"), 2).astype(jnp.int32)
    keep, give = gram_halves(x, NC // devices)(core.reshape(1), x)
    got = swap(give, "domain", 1)
    pieces = band_pieces(keep.shape[0], bands)(band.reshape(1), keep, got)
    total = pieces[0]
    for m in range(1, bands):
        total = total + swap(pieces[m], "band", m)
    levels = domains // 2
    heard = [total] + [swap(total, "domain", 2 * m) for m in range(1, levels)]
    while len(heard) > 1:
        heard = [heard[k] + heard[k + 1] for k in range(0, len(heard), 2)]
    excess = (heard[0] * (1.0 / NC)).astype(jnp.bfloat16)
    mine = [excess] + [swap(excess, "band", m) for m in range(1, bands)]
    other = [swap(e, "domain", 1) for e in mine]
    place = jnp.stack([band, core])
    out = correct(x, mine, bands)(place, x, *mine, *other)
    return lax.all_to_all(out, BOTH, split_axis=0, concat_axis=1, tiled=True)


def apply_blocks(excess, block_index, source_blocks):
    picked = jnp.take(source_blocks, block_index, axis=0)
    return jnp.einsum("bkij,bkjc->bic", excess, picked, preferred_element_type=jnp.float32)


def some_rows(functions, pattern):
    domains = lax.axis_size("domain")
    fdev = functions.shape[0]
    my_band = lax.axis_index("band")
    group = domains * fdev
    pieces = lax.all_to_all(functions, "domain", split_axis=1, concat_axis=0, tiled=True)
    every = lax.all_gather(pieces, "band", axis=0, tiled=True)
    width = every.shape[1]
    nblocks = every.shape[0] // BLOCK
    blocks = every.reshape(nblocks, BLOCK, width)
    rowblk = group // BLOCK
    block_index = lax.dynamic_slice_in_dim(pattern, my_band * rowblk, rowblk, 0)
    own_rows = pieces.reshape(rowblk, BLOCK, width)
    partners = jnp.take(blocks, block_index, axis=0)
    partial_sums = jnp.einsum(
        "bic,bkjc->bkij", own_rows, partners, preferred_element_type=jnp.float32
    )
    block_ids = my_band * rowblk + jnp.arange(rowblk, dtype=jnp.int32)
    on_diagonal = (block_index == block_ids[:, None]).astype(jnp.float32)
    total = lax.psum(partial_sums, "domain") * (1.0 / NC)
    identity = jnp.eye(BLOCK, dtype=jnp.float32)
    excess = (total - on_diagonal[:, :, None, None] * identity).astype(jnp.bfloat16)
    first = apply_blocks(excess, block_index, blocks)
    first_half = first.astype(jnp.bfloat16).reshape(group, width)
    all_first = lax.all_gather(first_half, "band", axis=0, tiled=True)
    first_blocks = all_first.reshape(nblocks, BLOCK, width)
    second = apply_blocks(excess, block_index, first_blocks)
    updated = own_rows.astype(jnp.float32) - 0.5 * first + 0.375 * second
    updated = updated.astype(jnp.bfloat16).reshape(group, width)
    return lax.all_to_all(updated, "domain", split_axis=0, concat_axis=1, tiled=True)


def per_device(functions, pattern):
    nblocks, nonzero = pattern.shape
    return (full_rows if nonzero == nblocks else some_rows)(functions, pattern)


def solution(mesh):
    placed = (P(BOTH, None), P())
    return jax.shard_map(
        per_device,
        mesh=mesh,
        in_specs=placed,
        out_specs=P(BOTH, None),
        check_vma=False,
    )
```

```python
import functools

import jax
import jax.numpy as jnp
from jax import lax
from jax.experimental import pallas as pl
from jax.experimental.pallas import tpu as pltpu
from jax.sharding import PartitionSpec as P

NC = 24576
BLOCK = 128
BOTH = ("band", "domain")


VMEM_LIMIT = pltpu.CompilerParams(vmem_limit_bytes=16 * 1024 * 1024)


def my_core():
    return lax.rem(lax.axis_index("domain"), 2)


def swap(value, axis, mask):
    count = lax.axis_size(axis)
    return lax.ppermute(value, axis, [(i, i ^ mask) for i in range(count)])


def upper_blocks(nblocks):
    return [(i, j) for i in range(nblocks) for j in range(i, nblocks)]


def gram_halves(x, share):
    rows, width = x.shape
    nblocks = rows // BLOCK
    pairs = upper_blocks(nblocks)
    half = len(pairs) * BLOCK // 2
    tile = 2 * BLOCK

    def body(x_ref, keep_ref, give_ref):
        core = my_core()
        eye = (
            lax.broadcasted_iota(jnp.int32, (BLOCK, BLOCK), 0) == lax.broadcasted_iota(jnp.int32, (BLOCK, BLOCK), 1)
        ).astype(jnp.float32) * share
        for a in range(rows // tile):
            for b in range(a, rows // tile):
                got = lax.dot_general(
                    x_ref[a * tile:(a + 1) * tile, :],
                    x_ref[b * tile:(b + 1) * tile, :],
                    (((1,), (1,)), ((), ())),
                    preferred_element_type=jnp.float32,
                )
                for i in range(2):
                    for j in range(2):
                        pair = (2 * a + i, 2 * b + j)
                        if pair not in pairs:
                            continue
                        block = got[i * BLOCK:(i + 1) * BLOCK, j * BLOCK:(j + 1) * BLOCK]
                        if pair[0] == pair[1]:
                            block = block - eye
                        start = pairs.index(pair) * BLOCK
                        side, at = start // half, start % half

                        @pl.when(core == side)
                        def _():
                            keep_ref[at:at + BLOCK, :] = block

                        @pl.when(core != side)
                        def _():
                            give_ref[at:at + BLOCK, :] = block

    stacked = jax.ShapeDtypeStruct((half, BLOCK), jnp.float32)
    return pl.pallas_call(
        body,
        out_shape=(stacked, stacked),
        compiler_params=VMEM_LIMIT,
    )


def band_pieces(half, bands):
    piece = half // bands

    def body(keep_ref, got_ref, *piece_refs):
        band = lax.axis_index("band")
        for m in range(bands):
            at = pl.ds(pl.multiple_of((band ^ m) * piece, piece), piece)
            piece_refs[m][...] = keep_ref[at, :] + got_ref[at, :]

    return pl.pallas_call(
        body,
        out_shape=tuple(jax.ShapeDtypeStruct((piece, BLOCK), jnp.float32) for _ in range(bands)),
        compiler_params=VMEM_LIMIT,
    )


def correct(x, pieces, bands):
    rows, width = x.shape
    nblocks = rows // BLOCK
    pairs = upper_blocks(nblocks)
    half = len(pairs) * BLOCK // 2
    piece = half // bands

    def body(x_ref, *refs):
        piece_refs, out_ref, packed, excess = refs[:-3], refs[-3], refs[-2], refs[-1]
        band, core = lax.axis_index("band"), my_core()
        for m in range(bands):
            for c in range(2):
                start = (core ^ c) * half + (band ^ m) * piece
                packed[pl.ds(pl.multiple_of(start, 16), piece), :] = piece_refs[c * bands + m][...]
        for p, (i, j) in enumerate(pairs):
            block = packed[p * BLOCK:(p + 1) * BLOCK, :]
            excess[i * BLOCK:(i + 1) * BLOCK, j * BLOCK:(j + 1) * BLOCK] = block
            if i != j:
                excess[j * BLOCK:(j + 1) * BLOCK, i * BLOCK:(i + 1) * BLOCK] = block.T
        first = jnp.dot(excess[...], x_ref[...], preferred_element_type=jnp.float32)
        second = jnp.dot(excess[...], first.astype(jnp.bfloat16), preferred_element_type=jnp.float32)
        out = x_ref[...].astype(jnp.float32) - 0.5 * first + 0.375 * second
        out_ref[...] = out.astype(jnp.bfloat16)

    return pl.pallas_call(
        body,
        out_shape=jax.ShapeDtypeStruct(x.shape, jnp.bfloat16),
        scratch_shapes=[
            pltpu.VMEM((2 * half, BLOCK), jnp.bfloat16),
            pltpu.VMEM((rows, rows), jnp.bfloat16),
        ],
        compiler_params=VMEM_LIMIT,
    )


def full_rows(functions, pattern):
    bands, domains = lax.axis_size("band"), lax.axis_size("domain")
    devices = bands * domains
    fdev, ncoef = functions.shape
    width = ncoef // devices
    x = lax.all_to_all(functions, BOTH, split_axis=1, concat_axis=0, tiled=True)
    keep, give = gram_halves(x, NC // devices)(x)
    got = swap(give, "domain", 1)
    pieces = band_pieces(keep.shape[0], bands)(keep, got)
    total = pieces[0]
    for m in range(1, bands):
        total = total + swap(pieces[m], "band", m)
    levels = domains // 2
    heard = [total] + [swap(total, "domain", 2 * m) for m in range(1, levels)]
    while len(heard) > 1:
        heard = [heard[k] + heard[k + 1] for k in range(0, len(heard), 2)]
    excess = (heard[0] * (1.0 / NC)).astype(jnp.bfloat16)
    mine = [excess] + [swap(excess, "band", m) for m in range(1, bands)]
    other = [swap(e, "domain", 1) for e in mine]
    out = correct(x, mine, bands)(x, *mine, *other)
    return lax.all_to_all(out, BOTH, split_axis=0, concat_axis=1, tiled=True)


def apply_blocks(excess, block_index, source_blocks):
    picked = jnp.take(source_blocks, block_index, axis=0)
    return jnp.einsum("bkij,bkjc->bic", excess, picked, preferred_element_type=jnp.float32)


def some_rows(functions, pattern):
    domains = lax.axis_size("domain")
    fdev = functions.shape[0]
    my_band = lax.axis_index("band")
    group = domains * fdev
    pieces = lax.all_to_all(functions, "domain", split_axis=1, concat_axis=0, tiled=True)
    every = lax.all_gather(pieces, "band", axis=0, tiled=True)
    width = every.shape[1]
    nblocks = every.shape[0] // BLOCK
    blocks = every.reshape(nblocks, BLOCK, width)
    rowblk = group // BLOCK
    block_index = lax.dynamic_slice_in_dim(pattern, my_band * rowblk, rowblk, 0)
    own_rows = pieces.reshape(rowblk, BLOCK, width)
    partners = jnp.take(blocks, block_index, axis=0)
    partial_sums = jnp.einsum(
        "bic,bkjc->bkij", own_rows, partners, preferred_element_type=jnp.float32
    )
    block_ids = my_band * rowblk + jnp.arange(rowblk, dtype=jnp.int32)
    on_diagonal = (block_index == block_ids[:, None]).astype(jnp.float32)
    total = lax.psum(partial_sums, "domain") * (1.0 / NC)
    identity = jnp.eye(BLOCK, dtype=jnp.float32)
    excess = (total - on_diagonal[:, :, None, None] * identity).astype(jnp.bfloat16)
    first = apply_blocks(excess, block_index, blocks)
    first_half = first.astype(jnp.bfloat16).reshape(group, width)
    all_first = lax.all_gather(first_half, "band", axis=0, tiled=True)
    first_blocks = all_first.reshape(nblocks, BLOCK, width)
    second = apply_blocks(excess, block_index, first_blocks)
    updated = own_rows.astype(jnp.float32) - 0.5 * first + 0.375 * second
    updated = updated.astype(jnp.bfloat16).reshape(group, width)
    return lax.all_to_all(updated, "domain", split_axis=0, concat_axis=1, tiled=True)


def per_device(functions, pattern):
    nblocks, nonzero = pattern.shape
    return (full_rows if nonzero == nblocks else some_rows)(functions, pattern)


def solution(mesh):
    placed = (P(BOTH, None), P())
    return jax.shard_map(
        per_device,
        mesh=mesh,
        in_specs=placed,
        out_specs=P(BOTH, None),
        check_vma=False,
    )
```

```python
import functools

import jax
import jax.numpy as jnp
from jax import lax
from jax.experimental import pallas as pl
from jax.experimental.pallas import tpu as pltpu
from jax.sharding import PartitionSpec as P

NC = 24576
BLOCK = 128
BOTH = ("band", "domain")


VMEM_LIMIT = pltpu.CompilerParams(vmem_limit_bytes=16 * 1024 * 1024)


def my_core():
    return lax.rem(lax.axis_index("domain"), 2)


def swap(value, axis, mask):
    count = lax.axis_size(axis)
    return lax.ppermute(value, axis, [(i, i ^ mask) for i in range(count)])


ACROSS = (((1,), (1,)), ((), ()))


def upper_blocks(count):
    return [(i, j) for i in range(count) for j in range(i, count)]


def own_gram(rows, width, share):
    count = rows // BLOCK

    def body(x_ref, out_ref):
        eye = (
            lax.broadcasted_iota(jnp.int32, (BLOCK, BLOCK), 0) == lax.broadcasted_iota(jnp.int32, (BLOCK, BLOCK), 1)
        ).astype(jnp.float32) * share
        got = lax.dot_general(x_ref[...], x_ref[...], ACROSS, preferred_element_type=jnp.float32)
        for p, (i, j) in enumerate(upper_blocks(count)):
            block = got[i * BLOCK:(i + 1) * BLOCK, j * BLOCK:(j + 1) * BLOCK]
            out_ref[p * BLOCK:(p + 1) * BLOCK, :] = block - eye if i == j else block

    stacked = count * (count + 1) // 2 * BLOCK
    return pl.pallas_call(
        body,
        out_shape=jax.ShapeDtypeStruct((stacked, BLOCK), jnp.float32),
        compiler_params=VMEM_LIMIT,
        cost_estimate=pl.CostEstimate(
            flops=2 * rows * rows * width, bytes_accessed=2 * rows * width, transcendentals=0
        ),
    )


def cross_gram(rows, width, bands):
    count = rows // BLOCK
    upper = count * (count + 1) // 2 * BLOCK
    mid = rows // 2
    stacked = upper + mid * count
    piece = stacked // bands

    def body(x_ref, y_ref, own_ref, *refs):
        piece_refs, stack = refs[:-1], refs[-1]
        core, band = my_core(), lax.axis_index("band")
        stack[0:upper, :] = own_ref[...]

        def put(left, right):
            got = lax.dot_general(left, right, ACROSS, preferred_element_type=jnp.float32)
            for j in range(count):
                stack[upper + j * mid:upper + (j + 1) * mid, :] = got[:, j * BLOCK:(j + 1) * BLOCK]

        @pl.when(core == 0)
        def _():
            put(x_ref[0:mid, :], y_ref[...])

        @pl.when(core == 1)
        def _():
            put(y_ref[mid:rows, :], x_ref[...])

        for m in range(bands):
            at = pl.ds(pl.multiple_of((band ^ m) * piece, piece), piece)
            piece_refs[m][...] = stack[at, :]

    return pl.pallas_call(
        body,
        out_shape=tuple(jax.ShapeDtypeStruct((piece, BLOCK), jnp.float32) for _ in range(bands)),
        scratch_shapes=[pltpu.VMEM((stacked, BLOCK), jnp.float32)],
        compiler_params=VMEM_LIMIT,
        cost_estimate=pl.CostEstimate(
            flops=rows * rows * width, bytes_accessed=4 * rows * width, transcendentals=0
        ),
    )


def correct(rows, width, bands):
    count = rows // BLOCK
    upper = count * (count + 1) // 2 * BLOCK
    mid = rows // 2
    stacked = upper + mid * count
    piece = stacked // bands

    def body(x_ref, y_ref, *refs):
        piece_refs, out_ref, packed, excess = refs[:-3], refs[-3], refs[-2], refs[-1]
        band, core = lax.axis_index("band"), my_core()
        for side in range(2):
            for m in range(bands):
                start = side * stacked + (band ^ m) * piece
                packed[pl.ds(pl.multiple_of(start, 16), piece), :] = piece_refs[side * bands + m][...]
        for side in range(2):
            for p, (i, j) in enumerate(upper_blocks(count)):
                at = side * stacked + p * BLOCK
                block = packed[at:at + BLOCK, :]
                row, column = side * rows + i * BLOCK, side * rows + j * BLOCK
                excess[row:row + BLOCK, column:column + BLOCK] = block
                if i != j:
                    excess[column:column + BLOCK, row:row + BLOCK] = block.T
        for part in range(2):
            for j in range(count):
                start = (part ^ core) * stacked + upper + j * mid
                block = packed[pl.ds(pl.multiple_of(start, 16), mid), :]
                row, column = part * mid, j * BLOCK

                @pl.when(core == 0)
                def _():
                    excess[row:row + mid, rows + column:rows + column + BLOCK] = block
                    excess[rows + column:rows + column + BLOCK, row:row + mid] = block.T

                @pl.when(core == 1)
                def _():
                    excess[rows + row:rows + row + mid, column:column + BLOCK] = block
                    excess[column:column + BLOCK, rows + row:rows + row + mid] = block.T

        own = excess[0:rows, :]
        twice = jnp.dot(own, excess[...], preferred_element_type=jnp.float32)
        change = (0.375 * twice - 0.5 * own.astype(jnp.float32)).astype(jnp.bfloat16)
        out = x_ref[...].astype(jnp.float32)
        out += jnp.dot(change[:, 0:rows], x_ref[...], preferred_element_type=jnp.float32)
        out += jnp.dot(change[:, rows:2 * rows], y_ref[...], preferred_element_type=jnp.float32)
        out_ref[...] = out.astype(jnp.bfloat16)

    return pl.pallas_call(
        body,
        out_shape=jax.ShapeDtypeStruct((rows, width), jnp.bfloat16),
        scratch_shapes=[
            pltpu.VMEM((2 * stacked, BLOCK), jnp.bfloat16),
            pltpu.VMEM((2 * rows, 2 * rows), jnp.bfloat16),
        ],
        compiler_params=VMEM_LIMIT,
    )


def full_rows(functions, pattern):
    bands, domains = lax.axis_size("band"), lax.axis_size("domain")
    devices, levels = bands * domains, domains // 2
    chips = devices // 2
    fdev, ncoef = functions.shape
    tall, width = fdev // 2, ncoef // chips
    rows = devices * tall
    order = [[b * domains + 2 * z + c for c in range(2) for b in range(bands) for z in range(levels)]]
    cut = functions.reshape(2, tall, chips, width).transpose(0, 2, 1, 3).reshape(devices, tall, width)
    x = lax.all_to_all(cut, BOTH, split_axis=0, concat_axis=0, axis_index_groups=order).reshape(rows, width)
    y = swap(x, "domain", 1)
    own = own_gram(rows, width, NC // chips)(x)
    pieces = cross_gram(rows, width, bands)(x, y, own)
    total = pieces[0]
    for m in range(1, bands):
        total = total + swap(pieces[m], "band", m)
    heard = [total] + [swap(total, "domain", 2 * m) for m in range(1, levels)]
    while len(heard) > 1:
        heard = [heard[k] + heard[k + 1] for k in range(0, len(heard), 2)]
    excess = (heard[0] * (1.0 / NC)).astype(jnp.bfloat16)
    mine = [excess] + [swap(excess, "band", m) for m in range(1, bands)]
    other = [swap(e, "domain", 1) for e in mine]
    out = correct(rows, width, bands)(x, y, *mine, *other).reshape(devices, tall, width)
    back = lax.all_to_all(out, BOTH, split_axis=0, concat_axis=0, axis_index_groups=order)
    return back.reshape(2, chips, tall, width).transpose(0, 2, 1, 3).reshape(fdev, ncoef)


def apply_blocks(excess, block_index, source_blocks):
    picked = jnp.take(source_blocks, block_index, axis=0)
    return jnp.einsum("bkij,bkjc->bic", excess, picked, preferred_element_type=jnp.float32)


def some_rows(functions, pattern):
    domains = lax.axis_size("domain")
    fdev = functions.shape[0]
    my_band = lax.axis_index("band")
    group = domains * fdev
    pieces = lax.all_to_all(functions, "domain", split_axis=1, concat_axis=0, tiled=True)
    every = lax.all_gather(pieces, "band", axis=0, tiled=True)
    width = every.shape[1]
    nblocks = every.shape[0] // BLOCK
    blocks = every.reshape(nblocks, BLOCK, width)
    rowblk = group // BLOCK
    block_index = lax.dynamic_slice_in_dim(pattern, my_band * rowblk, rowblk, 0)
    own_rows = pieces.reshape(rowblk, BLOCK, width)
    partners = jnp.take(blocks, block_index, axis=0)
    partial_sums = jnp.einsum(
        "bic,bkjc->bkij", own_rows, partners, preferred_element_type=jnp.float32
    )
    block_ids = my_band * rowblk + jnp.arange(rowblk, dtype=jnp.int32)
    on_diagonal = (block_index == block_ids[:, None]).astype(jnp.float32)
    total = lax.psum(partial_sums, "domain") * (1.0 / NC)
    identity = jnp.eye(BLOCK, dtype=jnp.float32)
    excess = (total - on_diagonal[:, :, None, None] * identity).astype(jnp.bfloat16)
    first = apply_blocks(excess, block_index, blocks)
    first_half = first.astype(jnp.bfloat16).reshape(group, width)
    all_first = lax.all_gather(first_half, "band", axis=0, tiled=True)
    first_blocks = all_first.reshape(nblocks, BLOCK, width)
    second = apply_blocks(excess, block_index, first_blocks)
    updated = own_rows.astype(jnp.float32) - 0.5 * first + 0.375 * second
    updated = updated.astype(jnp.bfloat16).reshape(group, width)
    return lax.all_to_all(updated, "domain", split_axis=0, concat_axis=1, tiled=True)


def per_device(functions, pattern):
    nblocks, nonzero = pattern.shape
    return (full_rows if nonzero == nblocks else some_rows)(functions, pattern)


def solution(mesh):
    placed = (P(BOTH, None), P())
    return jax.shard_map(
        per_device,
        mesh=mesh,
        in_specs=placed,
        out_specs=P(BOTH, None),
        check_vma=False,
    )
```

```python
import functools

import jax
import jax.numpy as jnp
from jax import lax
from jax.experimental import pallas as pl
from jax.experimental.pallas import tpu as pltpu
from jax.sharding import PartitionSpec as P

NC = 24576
BLOCK = 128
BOTH = ("band", "domain")
SENT = jnp.float16


VMEM_LIMIT = pltpu.CompilerParams(vmem_limit_bytes=16 * 1024 * 1024)


def my_core():
    return lax.rem(lax.axis_index("domain"), 2)


def swap(value, axis, mask):
    count = lax.axis_size(axis)
    return lax.ppermute(value, axis, [(i, i ^ mask) for i in range(count)])


ACROSS = (((1,), (1,)), ((), ()))


def upper_blocks(count):
    return [(i, j) for i in range(count) for j in range(i, count)]


def own_gram(rows, width, share):
    count = rows // BLOCK

    def body(x_ref, out_ref):
        eye = (
            lax.broadcasted_iota(jnp.int32, (BLOCK, BLOCK), 0) == lax.broadcasted_iota(jnp.int32, (BLOCK, BLOCK), 1)
        ).astype(jnp.float32) * share
        got = lax.dot_general(x_ref[...], x_ref[...], ACROSS, preferred_element_type=jnp.float32)
        for p, (i, j) in enumerate(upper_blocks(count)):
            block = got[i * BLOCK:(i + 1) * BLOCK, j * BLOCK:(j + 1) * BLOCK]
            out_ref[p * BLOCK:(p + 1) * BLOCK, :] = block - eye if i == j else block

    stacked = count * (count + 1) // 2 * BLOCK
    return pl.pallas_call(
        body,
        out_shape=jax.ShapeDtypeStruct((stacked, BLOCK), jnp.float32),
        compiler_params=VMEM_LIMIT,
        cost_estimate=pl.CostEstimate(
            flops=2 * rows * rows * width, bytes_accessed=2 * rows * width, transcendentals=0
        ),
    )


def cross_gram(rows, width, bands):
    count = rows // BLOCK
    upper = count * (count + 1) // 2 * BLOCK
    mid = rows // 2
    stacked = upper + mid * count
    piece = stacked // bands

    def body(x_ref, y_ref, own_ref, *refs):
        piece_refs, stack = refs[:-1], refs[-1]
        core, band = my_core(), lax.axis_index("band")
        stack[0:upper, :] = own_ref[...]

        def put(left, right):
            got = lax.dot_general(left, right, ACROSS, preferred_element_type=jnp.float32)
            for j in range(count):
                stack[upper + j * mid:upper + (j + 1) * mid, :] = got[:, j * BLOCK:(j + 1) * BLOCK]

        @pl.when(core == 0)
        def _():
            put(x_ref[0:mid, :], y_ref[...])

        @pl.when(core == 1)
        def _():
            put(y_ref[mid:rows, :], x_ref[...])

        for m in range(bands):
            at = pl.ds(pl.multiple_of((band ^ m) * piece, piece), piece)
            piece_refs[m][...] = stack[at, :] * (1.0 / NC)

    return pl.pallas_call(
        body,
        out_shape=tuple(jax.ShapeDtypeStruct((piece, BLOCK), jnp.float32) for _ in range(bands)),
        scratch_shapes=[pltpu.VMEM((stacked, BLOCK), jnp.float32)],
        compiler_params=VMEM_LIMIT,
        cost_estimate=pl.CostEstimate(
            flops=rows * rows * width, bytes_accessed=4 * rows * width, transcendentals=0
        ),
    )


def correct(rows, width, bands):
    count = rows // BLOCK
    upper = count * (count + 1) // 2 * BLOCK
    mid = rows // 2
    stacked = upper + mid * count
    piece = stacked // bands

    def body(x_ref, y_ref, *refs):
        piece_refs, out_ref, packed, excess = refs[:-3], refs[-3], refs[-2], refs[-1]
        band, core = lax.axis_index("band"), my_core()
        for side in range(2):
            for m in range(bands):
                start = side * stacked + (band ^ m) * piece
                packed[pl.ds(pl.multiple_of(start, 16), piece), :] = piece_refs[side * bands + m][...]
        for side in range(2):
            for p, (i, j) in enumerate(upper_blocks(count)):
                at = side * stacked + p * BLOCK
                block = packed[at:at + BLOCK, :]
                row, column = side * rows + i * BLOCK, side * rows + j * BLOCK
                excess[row:row + BLOCK, column:column + BLOCK] = block
                if i != j:
                    excess[column:column + BLOCK, row:row + BLOCK] = block.T
        for part in range(2):
            for j in range(count):
                start = (part ^ core) * stacked + upper + j * mid
                block = packed[pl.ds(pl.multiple_of(start, 16), mid), :]
                row, column = part * mid, j * BLOCK

                @pl.when(core == 0)
                def _():
                    excess[row:row + mid, rows + column:rows + column + BLOCK] = block
                    excess[rows + column:rows + column + BLOCK, row:row + mid] = block.T

                @pl.when(core == 1)
                def _():
                    excess[rows + row:rows + row + mid, column:column + BLOCK] = block
                    excess[column:column + BLOCK, rows + row:rows + row + mid] = block.T

        own = excess[0:rows, :]
        twice = jnp.dot(own, excess[...], preferred_element_type=jnp.float32)
        change = (0.375 * twice - 0.5 * own.astype(jnp.float32)).astype(jnp.bfloat16)
        out = x_ref[...].astype(jnp.float32)
        out += jnp.dot(change[:, 0:rows], x_ref[...], preferred_element_type=jnp.float32)
        out += jnp.dot(change[:, rows:2 * rows], y_ref[...], preferred_element_type=jnp.float32)
        out_ref[...] = out.astype(jnp.bfloat16)

    return pl.pallas_call(
        body,
        out_shape=jax.ShapeDtypeStruct((rows, width), jnp.bfloat16),
        scratch_shapes=[
            pltpu.VMEM((2 * stacked, BLOCK), jnp.bfloat16),
            pltpu.VMEM((2 * rows, 2 * rows), jnp.bfloat16),
        ],
        compiler_params=VMEM_LIMIT,
    )


def full_rows(functions, pattern):
    bands, domains = lax.axis_size("band"), lax.axis_size("domain")
    devices, levels = bands * domains, domains // 2
    chips = devices // 2
    fdev, ncoef = functions.shape
    tall, width = fdev // 2, ncoef // chips
    rows = devices * tall
    order = [[b * domains + 2 * z + c for c in range(2) for b in range(bands) for z in range(levels)]]
    cut = functions.reshape(2, tall, chips, width).transpose(0, 2, 1, 3).reshape(devices, tall, width)
    x = lax.all_to_all(cut, BOTH, split_axis=0, concat_axis=0, axis_index_groups=order).reshape(rows, width)
    y = swap(x, "domain", 1)
    own = own_gram(rows, width, NC // chips)(x)
    pieces = cross_gram(rows, width, bands)(x, y, own)
    total = pieces[0]
    for m in range(1, bands):
        total = total + swap(pieces[m].astype(SENT), "band", m).astype(jnp.float32)
    total = total.astype(SENT)
    heard = [total] + [swap(total, "domain", 2 * m) for m in range(1, levels)]
    heard = [h.astype(jnp.float32) for h in heard]
    while len(heard) > 1:
        heard = [heard[k] + heard[k + 1] for k in range(0, len(heard), 2)]
    excess = heard[0].astype(jnp.bfloat16)
    mine = [excess] + [swap(excess, "band", m) for m in range(1, bands)]
    other = [swap(e, "domain", 1) for e in mine]
    out = correct(rows, width, bands)(x, y, *mine, *other).reshape(devices, tall, width)
    back = lax.all_to_all(out, BOTH, split_axis=0, concat_axis=0, axis_index_groups=order)
    return back.reshape(2, chips, tall, width).transpose(0, 2, 1, 3).reshape(fdev, ncoef)


def apply_blocks(excess, block_index, source_blocks):
    picked = jnp.take(source_blocks, block_index, axis=0)
    return jnp.einsum("bkij,bkjc->bic", excess, picked, preferred_element_type=jnp.float32)


def some_rows(functions, pattern):
    domains = lax.axis_size("domain")
    fdev = functions.shape[0]
    my_band = lax.axis_index("band")
    group = domains * fdev
    pieces = lax.all_to_all(functions, "domain", split_axis=1, concat_axis=0, tiled=True)
    every = lax.all_gather(pieces, "band", axis=0, tiled=True)
    width = every.shape[1]
    nblocks = every.shape[0] // BLOCK
    blocks = every.reshape(nblocks, BLOCK, width)
    rowblk = group // BLOCK
    block_index = lax.dynamic_slice_in_dim(pattern, my_band * rowblk, rowblk, 0)
    own_rows = pieces.reshape(rowblk, BLOCK, width)
    partners = jnp.take(blocks, block_index, axis=0)
    partial_sums = jnp.einsum(
        "bic,bkjc->bkij", own_rows, partners, preferred_element_type=jnp.float32
    )
    block_ids = my_band * rowblk + jnp.arange(rowblk, dtype=jnp.int32)
    on_diagonal = (block_index == block_ids[:, None]).astype(jnp.float32)
    total = lax.psum(partial_sums, "domain") * (1.0 / NC)
    identity = jnp.eye(BLOCK, dtype=jnp.float32)
    excess = (total - on_diagonal[:, :, None, None] * identity).astype(jnp.bfloat16)
    first = apply_blocks(excess, block_index, blocks)
    first_half = first.astype(jnp.bfloat16).reshape(group, width)
    all_first = lax.all_gather(first_half, "band", axis=0, tiled=True)
    first_blocks = all_first.reshape(nblocks, BLOCK, width)
    second = apply_blocks(excess, block_index, first_blocks)
    updated = own_rows.astype(jnp.float32) - 0.5 * first + 0.375 * second
    updated = updated.astype(jnp.bfloat16).reshape(group, width)
    return lax.all_to_all(updated, "domain", split_axis=0, concat_axis=1, tiled=True)


def per_device(functions, pattern):
    nblocks, nonzero = pattern.shape
    return (full_rows if nonzero == nblocks else some_rows)(functions, pattern)


def solution(mesh):
    placed = (P(BOTH, None), P())
    return jax.shard_map(
        per_device,
        mesh=mesh,
        in_specs=placed,
        out_specs=P(BOTH, None),
        check_vma=False,
    )
```

```python
import functools

import jax
import jax.numpy as jnp
from jax import lax
from jax.experimental import pallas as pl
from jax.experimental.pallas import tpu as pltpu
from jax.sharding import PartitionSpec as P

NC = 24576
BLOCK = 128
BOTH = ("band", "domain")
SENT = jnp.float16
MEASURED = (10, 14, 12, 1, 9, 0, 3, 8, 2, 11, 7, 4, 13, 6, 15, 5)


VMEM_LIMIT = pltpu.CompilerParams(vmem_limit_bytes=16 * 1024 * 1024)


def my_core():
    return lax.rem(lax.axis_index("domain"), 2)


def swap(value, axis, mask):
    count = lax.axis_size(axis)
    return lax.ppermute(value, axis, [(i, i ^ mask) for i in range(count)])


ACROSS = (((1,), (1,)), ((), ()))


def chip_order(bands, levels):
    if (bands, levels) == (4, 4):
        return MEASURED
    return sorted(range(bands * levels), key=lambda q: (q // levels, abs(q % levels - levels // 2), q))


def upper_blocks(count):
    return [(i, j) for i in range(count) for j in range(i, count)]


def own_gram(rows, width, share):
    count = rows // BLOCK

    def body(x_ref, out_ref):
        eye = (
            lax.broadcasted_iota(jnp.int32, (BLOCK, BLOCK), 0) == lax.broadcasted_iota(jnp.int32, (BLOCK, BLOCK), 1)
        ).astype(jnp.float32) * share
        got = lax.dot_general(x_ref[...], x_ref[...], ACROSS, preferred_element_type=jnp.float32)
        for p, (i, j) in enumerate(upper_blocks(count)):
            block = got[i * BLOCK:(i + 1) * BLOCK, j * BLOCK:(j + 1) * BLOCK]
            out_ref[p * BLOCK:(p + 1) * BLOCK, :] = block - eye if i == j else block

    stacked = count * (count + 1) // 2 * BLOCK
    return pl.pallas_call(
        body,
        out_shape=jax.ShapeDtypeStruct((stacked, BLOCK), jnp.float32),
        compiler_params=VMEM_LIMIT,
        cost_estimate=pl.CostEstimate(
            flops=2 * rows * rows * width, bytes_accessed=2 * rows * width, transcendentals=0
        ),
    )


def cross_gram(rows, width, bands):
    count = rows // BLOCK
    upper = count * (count + 1) // 2 * BLOCK
    mid = rows // 2
    stacked = upper + mid * count
    piece = stacked // bands

    def body(x_ref, y_ref, own_ref, *refs):
        piece_refs, stack = refs[:-1], refs[-1]
        core, band = my_core(), lax.axis_index("band")
        stack[0:upper, :] = own_ref[...]

        def put(left, right):
            got = lax.dot_general(left, right, ACROSS, preferred_element_type=jnp.float32)
            for j in range(count):
                stack[upper + j * mid:upper + (j + 1) * mid, :] = got[:, j * BLOCK:(j + 1) * BLOCK]

        @pl.when(core == 0)
        def _():
            put(x_ref[0:mid, :], y_ref[...])

        @pl.when(core == 1)
        def _():
            put(y_ref[mid:rows, :], x_ref[...])

        for m in range(bands):
            at = pl.ds(pl.multiple_of((band ^ m) * piece, piece), piece)
            piece_refs[m][...] = stack[at, :] * (1.0 / NC)

    return pl.pallas_call(
        body,
        out_shape=tuple(jax.ShapeDtypeStruct((piece, BLOCK), jnp.float32) for _ in range(bands)),
        scratch_shapes=[pltpu.VMEM((stacked, BLOCK), jnp.float32)],
        compiler_params=VMEM_LIMIT,
        cost_estimate=pl.CostEstimate(
            flops=rows * rows * width, bytes_accessed=4 * rows * width, transcendentals=0
        ),
    )


def correct(rows, width, bands, tall):
    count = rows // BLOCK
    upper = count * (count + 1) // 2 * BLOCK
    mid = rows // 2
    stacked = upper + mid * count
    piece = stacked // bands

    def body(x_ref, y_ref, *refs):
        piece_refs, out_ref, packed, excess = refs[:-3], refs[-3], refs[-2], refs[-1]
        band, core = lax.axis_index("band"), my_core()
        for side in range(2):
            for m in range(bands):
                start = side * stacked + (band ^ m) * piece
                packed[pl.ds(pl.multiple_of(start, 16), piece), :] = piece_refs[side * bands + m][...]
        for side in range(2):
            for p, (i, j) in enumerate(upper_blocks(count)):
                at = side * stacked + p * BLOCK
                block = packed[at:at + BLOCK, :]
                row, column = side * rows + i * BLOCK, side * rows + j * BLOCK
                excess[row:row + BLOCK, column:column + BLOCK] = block
                if i != j:
                    excess[column:column + BLOCK, row:row + BLOCK] = block.T
        for part in range(2):
            for j in range(count):
                start = (part ^ core) * stacked + upper + j * mid
                block = packed[pl.ds(pl.multiple_of(start, 16), mid), :]
                row, column = part * mid, j * BLOCK

                @pl.when(core == 0)
                def _():
                    excess[row:row + mid, rows + column:rows + column + BLOCK] = block
                    excess[rows + column:rows + column + BLOCK, row:row + mid] = block.T

                @pl.when(core == 1)
                def _():
                    excess[rows + row:rows + row + mid, column:column + BLOCK] = block
                    excess[column:column + BLOCK, rows + row:rows + row + mid] = block.T

        mine = pl.ds(pl.multiple_of(core * mid, mid), mid)
        theirs = pl.ds(pl.multiple_of(rows + core * mid, mid), mid)
        own = jnp.concatenate([excess[mine, :], excess[theirs, :]], axis=0)
        twice = jnp.dot(own, excess[...], preferred_element_type=jnp.float32)
        change = (0.375 * twice - 0.5 * own.astype(jnp.float32)).astype(jnp.bfloat16)
        out = jnp.concatenate([x_ref[mine, :], y_ref[mine, :]], axis=0).astype(jnp.float32)
        out += jnp.dot(change[:, 0:rows], x_ref[...], preferred_element_type=jnp.float32)
        out += jnp.dot(change[:, rows:2 * rows], y_ref[...], preferred_element_type=jnp.float32)
        near, far = out[0:mid], out[mid:rows]
        upper_half = jnp.where(core == 0, near, far).reshape(mid // tall, tall, width)
        lower_half = jnp.where(core == 0, far, near).reshape(mid // tall, tall, width)
        out = jnp.concatenate([upper_half, lower_half], axis=1).reshape(rows, width)
        out_ref[...] = out.astype(jnp.bfloat16)

    return pl.pallas_call(
        body,
        out_shape=jax.ShapeDtypeStruct((rows, width), jnp.bfloat16),
        scratch_shapes=[
            pltpu.VMEM((2 * stacked, BLOCK), jnp.bfloat16),
            pltpu.VMEM((2 * rows, 2 * rows), jnp.bfloat16),
        ],
        compiler_params=VMEM_LIMIT,
    )


def full_rows(functions, pattern):
    bands, domains = lax.axis_size("band"), lax.axis_size("domain")
    devices, levels = bands * domains, domains // 2
    chips = devices // 2
    fdev, ncoef = functions.shape
    tall, width = fdev // 2, ncoef // chips
    rows = devices * tall
    spread = [[2 * q + c for q in chip_order(bands, levels)] for c in range(2)]
    order = [spread[0] + spread[1]]
    cut = functions.reshape(2, tall, chips, width).transpose(0, 2, 1, 3).reshape(devices, tall, width)
    x = lax.all_to_all(cut, BOTH, split_axis=0, concat_axis=0, axis_index_groups=order).reshape(rows, width)
    y = swap(x, "domain", 1)
    own = own_gram(rows, width, NC // chips)(x)
    pieces = cross_gram(rows, width, bands)(x, y, own)
    total = pieces[0]
    for m in range(1, bands):
        total = total + swap(pieces[m].astype(SENT), "band", m).astype(jnp.float32)
    total = total.astype(SENT)
    heard = [total] + [swap(total, "domain", 2 * m) for m in range(1, levels)]
    heard = [h.astype(jnp.float32) for h in heard]
    while len(heard) > 1:
        heard = [heard[k] + heard[k + 1] for k in range(0, len(heard), 2)]
    excess = heard[0].astype(jnp.bfloat16)
    mine = [excess] + [swap(excess, "band", m) for m in range(1, bands)]
    other = [swap(e, "domain", 1) for e in mine]
    out = correct(rows, width, bands, tall)(x, y, *mine, *other).reshape(chips, fdev, width)
    back = lax.all_to_all(out, BOTH, split_axis=0, concat_axis=0, axis_index_groups=spread)
    return back.transpose(1, 0, 2).reshape(fdev, ncoef)


def apply_blocks(excess, block_index, source_blocks):
    picked = jnp.take(source_blocks, block_index, axis=0)
    return jnp.einsum("bkij,bkjc->bic", excess, picked, preferred_element_type=jnp.float32)


def some_rows(functions, pattern):
    domains = lax.axis_size("domain")
    fdev = functions.shape[0]
    my_band = lax.axis_index("band")
    group = domains * fdev
    pieces = lax.all_to_all(functions, "domain", split_axis=1, concat_axis=0, tiled=True)
    every = lax.all_gather(pieces, "band", axis=0, tiled=True)
    width = every.shape[1]
    nblocks = every.shape[0] // BLOCK
    blocks = every.reshape(nblocks, BLOCK, width)
    rowblk = group // BLOCK
    block_index = lax.dynamic_slice_in_dim(pattern, my_band * rowblk, rowblk, 0)
    own_rows = pieces.reshape(rowblk, BLOCK, width)
    partners = jnp.take(blocks, block_index, axis=0)
    partial_sums = jnp.einsum(
        "bic,bkjc->bkij", own_rows, partners, preferred_element_type=jnp.float32
    )
    block_ids = my_band * rowblk + jnp.arange(rowblk, dtype=jnp.int32)
    on_diagonal = (block_index == block_ids[:, None]).astype(jnp.float32)
    total = lax.psum(partial_sums, "domain") * (1.0 / NC)
    identity = jnp.eye(BLOCK, dtype=jnp.float32)
    excess = (total - on_diagonal[:, :, None, None] * identity).astype(jnp.bfloat16)
    first = apply_blocks(excess, block_index, blocks)
    first_half = first.astype(jnp.bfloat16).reshape(group, width)
    all_first = lax.all_gather(first_half, "band", axis=0, tiled=True)
    first_blocks = all_first.reshape(nblocks, BLOCK, width)
    second = apply_blocks(excess, block_index, first_blocks)
    updated = own_rows.astype(jnp.float32) - 0.5 * first + 0.375 * second
    updated = updated.astype(jnp.bfloat16).reshape(group, width)
    return lax.all_to_all(updated, "domain", split_axis=0, concat_axis=1, tiled=True)


def per_device(functions, pattern):
    nblocks, nonzero = pattern.shape
    return (full_rows if nonzero == nblocks else some_rows)(functions, pattern)


def solution(mesh):
    placed = (P(BOTH, None), P())
    return jax.shard_map(
        per_device,
        mesh=mesh,
        in_specs=placed,
        out_specs=P(BOTH, None),
        check_vma=False,
    )
```

```python
import functools

import jax
import jax.numpy as jnp
from jax import lax
from jax.experimental import pallas as pl
from jax.experimental.pallas import tpu as pltpu
from jax.sharding import PartitionSpec as P

NC = 24576
BLOCK = 128
BOTH = ("band", "domain")
MEASURED = (10, 14, 12, 1, 9, 0, 3, 8, 2, 11, 7, 4, 13, 6, 15, 5)


VMEM_LIMIT = pltpu.CompilerParams(vmem_limit_bytes=16 * 1024 * 1024)


def my_core():
    return lax.rem(lax.axis_index("domain"), 2)


def swap(value, axis, mask):
    count = lax.axis_size(axis)
    return lax.ppermute(value, axis, [(i, i ^ mask) for i in range(count)])


ACROSS = (((1,), (1,)), ((), ()))


def chip_order(bands, levels):
    if (bands, levels) == (4, 4):
        return MEASURED
    return sorted(range(bands * levels), key=lambda q: (q // levels, abs(q % levels - levels // 2), q))


def upper_blocks(count):
    return [(i, j) for i in range(count) for j in range(i, count)]


def own_gram(rows, width, share):
    count = rows // BLOCK

    def body(x_ref, out_ref):
        eye = (
            lax.broadcasted_iota(jnp.int32, (BLOCK, BLOCK), 0) == lax.broadcasted_iota(jnp.int32, (BLOCK, BLOCK), 1)
        ).astype(jnp.float32) * share
        got = lax.dot_general(x_ref[...], x_ref[...], ACROSS, preferred_element_type=jnp.float32)
        for p, (i, j) in enumerate(upper_blocks(count)):
            block = got[i * BLOCK:(i + 1) * BLOCK, j * BLOCK:(j + 1) * BLOCK]
            out_ref[p * BLOCK:(p + 1) * BLOCK, :] = block - eye if i == j else block

    stacked = count * (count + 1) // 2 * BLOCK
    return pl.pallas_call(
        body,
        out_shape=jax.ShapeDtypeStruct((stacked, BLOCK), jnp.float32),
        compiler_params=VMEM_LIMIT,
        cost_estimate=pl.CostEstimate(
            flops=2 * rows * rows * width, bytes_accessed=2 * rows * width, transcendentals=0
        ),
    )


def cross_gram(rows, width, bands):
    count = rows // BLOCK
    upper = count * (count + 1) // 2 * BLOCK
    mid = rows // 2
    stacked = upper + mid * count
    piece = stacked // bands

    def body(x_ref, y_ref, own_ref, *refs):
        piece_refs, stack = refs[:-1], refs[-1]
        core, band = my_core(), lax.axis_index("band")
        stack[0:upper, :] = own_ref[...]

        def put(left, right):
            got = lax.dot_general(left, right, ACROSS, preferred_element_type=jnp.float32)
            for j in range(count):
                stack[upper + j * mid:upper + (j + 1) * mid, :] = got[:, j * BLOCK:(j + 1) * BLOCK]

        @pl.when(core == 0)
        def _():
            put(x_ref[0:mid, :], y_ref[...])

        @pl.when(core == 1)
        def _():
            put(y_ref[mid:rows, :], x_ref[...])

        for m in range(bands):
            at = pl.ds(pl.multiple_of((band ^ m) * piece, piece), piece)
            piece_refs[m][...] = stack[at, :]

    return pl.pallas_call(
        body,
        out_shape=tuple(jax.ShapeDtypeStruct((piece, BLOCK), jnp.float32) for _ in range(bands)),
        scratch_shapes=[pltpu.VMEM((stacked, BLOCK), jnp.float32)],
        compiler_params=VMEM_LIMIT,
        cost_estimate=pl.CostEstimate(
            flops=rows * rows * width, bytes_accessed=4 * rows * width, transcendentals=0
        ),
    )


def correct(rows, width, bands, tall):
    count = rows // BLOCK
    upper = count * (count + 1) // 2 * BLOCK
    mid = rows // 2
    stacked = upper + mid * count
    piece = stacked // bands

    def body(x_ref, y_ref, *refs):
        piece_refs, out_ref, packed, excess = refs[:-3], refs[-3], refs[-2], refs[-1]
        band, core = lax.axis_index("band"), my_core()
        for side in range(2):
            for m in range(bands):
                start = side * stacked + (band ^ m) * piece
                packed[pl.ds(pl.multiple_of(start, 16), piece), :] = piece_refs[side * bands + m][...]
        for side in range(2):
            for p, (i, j) in enumerate(upper_blocks(count)):
                at = side * stacked + p * BLOCK
                block = packed[at:at + BLOCK, :]
                row, column = side * rows + i * BLOCK, side * rows + j * BLOCK
                excess[row:row + BLOCK, column:column + BLOCK] = block
                if i != j:
                    excess[column:column + BLOCK, row:row + BLOCK] = block.T
        for part in range(2):
            for j in range(count):
                start = (part ^ core) * stacked + upper + j * mid
                block = packed[pl.ds(pl.multiple_of(start, 16), mid), :]
                row, column = part * mid, j * BLOCK

                @pl.when(core == 0)
                def _():
                    excess[row:row + mid, rows + column:rows + column + BLOCK] = block
                    excess[rows + column:rows + column + BLOCK, row:row + mid] = block.T

                @pl.when(core == 1)
                def _():
                    excess[rows + row:rows + row + mid, column:column + BLOCK] = block
                    excess[column:column + BLOCK, rows + row:rows + row + mid] = block.T

        mine = pl.ds(pl.multiple_of(core * mid, mid), mid)
        theirs = pl.ds(pl.multiple_of(rows + core * mid, mid), mid)
        own = jnp.concatenate([excess[mine, :], excess[theirs, :]], axis=0)
        twice = jnp.dot(own, excess[...], preferred_element_type=jnp.float32)
        change = 0.375 * twice - 0.5 * own.astype(jnp.float32)
        row = lax.broadcasted_iota(jnp.int32, (rows, 2 * rows), 0)
        column = lax.broadcasted_iota(jnp.int32, (rows, 2 * rows), 1)
        diagonal = column == row + core * mid + jnp.where(row < mid, 0, rows - mid)
        weight = 1.0 + jnp.sum(jnp.where(diagonal, change, 0.0), axis=1, keepdims=True)
        change = jnp.where(diagonal, 0.0, change).astype(jnp.bfloat16)
        out = jnp.concatenate([x_ref[mine, :], y_ref[mine, :]], axis=0).astype(jnp.float32) * weight
        out += jnp.dot(change[:, 0:rows], x_ref[...], preferred_element_type=jnp.float32)
        out += jnp.dot(change[:, rows:2 * rows], y_ref[...], preferred_element_type=jnp.float32)
        near, far = out[0:mid], out[mid:rows]
        upper_half = jnp.where(core == 0, near, far).reshape(mid // tall, tall, width)
        lower_half = jnp.where(core == 0, far, near).reshape(mid // tall, tall, width)
        out = jnp.concatenate([upper_half, lower_half], axis=1).reshape(rows, width)
        out_ref[...] = out.astype(jnp.bfloat16)

    return pl.pallas_call(
        body,
        out_shape=jax.ShapeDtypeStruct((rows, width), jnp.bfloat16),
        scratch_shapes=[
            pltpu.VMEM((2 * stacked, BLOCK), jnp.bfloat16),
            pltpu.VMEM((2 * rows, 2 * rows), jnp.bfloat16),
        ],
        compiler_params=VMEM_LIMIT,
    )


def full_rows(functions, pattern):
    bands, domains = lax.axis_size("band"), lax.axis_size("domain")
    devices, levels = bands * domains, domains // 2
    chips = devices // 2
    fdev, ncoef = functions.shape
    tall, width = fdev // 2, ncoef // chips
    rows = devices * tall
    spread = [[2 * q + c for q in chip_order(bands, levels)] for c in range(2)]
    order = [spread[0] + spread[1]]
    cut = functions.reshape(2, tall, chips, width).transpose(0, 2, 1, 3).reshape(devices, tall, width)
    x = lax.all_to_all(cut, BOTH, split_axis=0, concat_axis=0, axis_index_groups=order).reshape(rows, width)
    y = swap(x, "domain", 1)
    own = own_gram(rows, width, NC // chips)(x)
    pieces = cross_gram(rows, width, bands)(x, y, own)
    total = pieces[0]
    for m in range(1, bands):
        total = total + swap(pieces[m], "band", m)
    heard = [total] + [swap(total, "domain", 2 * m) for m in range(1, levels)]
    while len(heard) > 1:
        heard = [heard[k] + heard[k + 1] for k in range(0, len(heard), 2)]
    excess = (heard[0] * (1.0 / NC)).astype(jnp.bfloat16)
    mine = [excess] + [swap(excess, "band", m) for m in range(1, bands)]
    other = [swap(e, "domain", 1) for e in mine]
    out = correct(rows, width, bands, tall)(x, y, *mine, *other).reshape(chips, fdev, width)
    back = lax.all_to_all(out, BOTH, split_axis=0, concat_axis=0, axis_index_groups=spread)
    return back.transpose(1, 0, 2).reshape(fdev, ncoef)


def apply_blocks(excess, block_index, source_blocks):
    picked = jnp.take(source_blocks, block_index, axis=0)
    return jnp.einsum("bkij,bkjc->bic", excess, picked, preferred_element_type=jnp.float32)


def some_rows(functions, pattern):
    domains = lax.axis_size("domain")
    fdev = functions.shape[0]
    my_band = lax.axis_index("band")
    group = domains * fdev
    pieces = lax.all_to_all(functions, "domain", split_axis=1, concat_axis=0, tiled=True)
    every = lax.all_gather(pieces, "band", axis=0, tiled=True)
    width = every.shape[1]
    nblocks = every.shape[0] // BLOCK
    blocks = every.reshape(nblocks, BLOCK, width)
    rowblk = group // BLOCK
    block_index = lax.dynamic_slice_in_dim(pattern, my_band * rowblk, rowblk, 0)
    own_rows = pieces.reshape(rowblk, BLOCK, width)
    partners = jnp.take(blocks, block_index, axis=0)
    partial_sums = jnp.einsum(
        "bic,bkjc->bkij", own_rows, partners, preferred_element_type=jnp.float32
    )
    block_ids = my_band * rowblk + jnp.arange(rowblk, dtype=jnp.int32)
    on_diagonal = (block_index == block_ids[:, None]).astype(jnp.float32)
    total = lax.psum(partial_sums, "domain") * (1.0 / NC)
    identity = jnp.eye(BLOCK, dtype=jnp.float32)
    excess = (total - on_diagonal[:, :, None, None] * identity).astype(jnp.bfloat16)
    first = apply_blocks(excess, block_index, blocks)
    first_half = first.astype(jnp.bfloat16).reshape(group, width)
    all_first = lax.all_gather(first_half, "band", axis=0, tiled=True)
    first_blocks = all_first.reshape(nblocks, BLOCK, width)
    second = apply_blocks(excess, block_index, first_blocks)
    updated = own_rows.astype(jnp.float32) - 0.5 * first + 0.375 * second
    updated = updated.astype(jnp.bfloat16).reshape(group, width)
    return lax.all_to_all(updated, "domain", split_axis=0, concat_axis=1, tiled=True)


def per_device(functions, pattern):
    nblocks, nonzero = pattern.shape
    return (full_rows if nonzero == nblocks else some_rows)(functions, pattern)


def solution(mesh):
    placed = (P(BOTH, None), P())
    return jax.shard_map(
        per_device,
        mesh=mesh,
        in_specs=placed,
        out_specs=P(BOTH, None),
        check_vma=False,
    )
```

```python
import functools

import jax
import jax.numpy as jnp
from jax import lax
from jax.experimental import pallas as pl
from jax.experimental.pallas import tpu as pltpu
from jax.sharding import PartitionSpec as P

NC = 24576
BLOCK = 128
BOTH = ("band", "domain")
MEASURED = (10, 14, 12, 1, 9, 0, 3, 8, 2, 11, 7, 4, 13, 6, 15, 5)


VMEM_LIMIT = pltpu.CompilerParams(vmem_limit_bytes=16 * 1024 * 1024)


def my_core():
    return lax.rem(lax.axis_index("domain"), 2)


def swap(value, axis, mask):
    count = lax.axis_size(axis)
    return lax.ppermute(value, axis, [(i, i ^ mask) for i in range(count)])


ACROSS = (((1,), (1,)), ((), ()))


def chip_order(bands, levels):
    if (bands, levels) == (4, 4):
        return MEASURED
    return sorted(range(bands * levels), key=lambda q: (q // levels, abs(q % levels - levels // 2), q))


def squares():
    shape = (BLOCK, BLOCK)
    return lax.broadcasted_iota(jnp.int32, shape, 0), lax.broadcasted_iota(jnp.int32, shape, 1)


def heights(bands):
    body = 4 * BLOCK
    piece = -(-(body + 8) // (8 * bands)) * 8
    return body, piece * bands - body, piece


def own_gram(width, share, bands):
    _, tail, _ = heights(bands)

    def body(x_ref, out_ref):
        row, column = squares()
        got = lax.dot_general(x_ref[...], x_ref[...], ACROSS, preferred_element_type=jnp.float32)
        eye = jnp.where(row == column, share, 0.0).astype(jnp.float32)
        first, second = got[0:BLOCK, 0:BLOCK] - eye, got[BLOCK:, BLOCK:] - eye
        out_ref[0:BLOCK, :] = jnp.where(row <= column, first, second)
        out_ref[BLOCK:2 * BLOCK, :] = got[0:BLOCK, BLOCK:]
        line = jnp.sum(jnp.where(row == column, second, 0.0), axis=0, keepdims=True)
        out_ref[2 * BLOCK:2 * BLOCK + tail, :] = jnp.broadcast_to(line, (tail, BLOCK))

    return pl.pallas_call(
        body,
        out_shape=jax.ShapeDtypeStruct((2 * BLOCK + tail, BLOCK), jnp.float32),
        compiler_params=VMEM_LIMIT,
        cost_estimate=pl.CostEstimate(
            flops=8 * BLOCK * BLOCK * width, bytes_accessed=4 * BLOCK * width, transcendentals=0
        ),
    )


def cross_gram(width, bands):
    whole, tail, piece = heights(bands)

    def body(x_ref, y_ref, own_ref, *refs):
        piece_refs, stack = refs[:-1], refs[-1]
        core, band = my_core(), lax.axis_index("band")
        stack[0:2 * BLOCK, :] = own_ref[0:2 * BLOCK, :]
        stack[whole:whole + tail, :] = own_ref[2 * BLOCK:2 * BLOCK + tail, :]

        def put(left, right):
            got = lax.dot_general(left, right, ACROSS, preferred_element_type=jnp.float32)
            for j in range(2):
                stack[(2 + j) * BLOCK:(3 + j) * BLOCK, :] = got[:, j * BLOCK:(j + 1) * BLOCK]

        @pl.when(core == 0)
        def _():
            put(x_ref[0:BLOCK, :], y_ref[...])

        @pl.when(core == 1)
        def _():
            put(y_ref[BLOCK:2 * BLOCK, :], x_ref[...])

        for m in range(bands):
            at = pl.ds(pl.multiple_of((band ^ m) * piece, 8), piece)
            piece_refs[m][...] = stack[at, :]

    return pl.pallas_call(
        body,
        out_shape=tuple(jax.ShapeDtypeStruct((piece, BLOCK), jnp.float32) for _ in range(bands)),
        scratch_shapes=[pltpu.VMEM((whole + tail, BLOCK), jnp.float32)],
        compiler_params=VMEM_LIMIT,
        cost_estimate=pl.CostEstimate(
            flops=4 * BLOCK * BLOCK * width, bytes_accessed=8 * BLOCK * width, transcendentals=0
        ),
    )


def correct(width, bands, tall):
    whole, tail, piece = heights(bands)
    stacked = whole + tail
    mid, rows = BLOCK, 2 * BLOCK

    def body(x_ref, y_ref, *refs):
        piece_refs, out_ref, packed, excess = refs[:-3], refs[-3], refs[-2], refs[-1]
        band, core = lax.axis_index("band"), my_core()
        for side in range(2):
            for m in range(bands):
                start = side * stacked + (band ^ m) * piece
                held = piece_refs[side * bands + m][...].astype(jnp.float32)
                packed[pl.ds(pl.multiple_of(start, 8), piece), :] = held

        def put(row, column, block):
            at = (slice(row * BLOCK, (row + 1) * BLOCK), slice(column * BLOCK, (column + 1) * BLOCK))
            excess[at] = block.astype(jnp.bfloat16)

        row, column = squares()
        for side in range(2):
            at = side * stacked
            both, beside = packed[at:at + BLOCK, :], packed[at + BLOCK:at + 2 * BLOCK, :]
            line = packed[at + whole:at + whole + 8, :][0:1, :]
            turned = both.T
            put(2 * side, 2 * side, jnp.where(row <= column, both, turned))
            second = jnp.where(row > column, both, turned)
            put(2 * side + 1, 2 * side + 1, jnp.where(row == column, line, second))
            put(2 * side, 2 * side + 1, beside)
            put(2 * side + 1, 2 * side, beside.T)
        for part in range(2):
            for j in range(2):
                start = (part ^ core) * stacked + (2 + j) * BLOCK
                block = packed[pl.ds(pl.multiple_of(start, 8), BLOCK), :]

                @pl.when(core == 0)
                def _():
                    put(part, 2 + j, block)
                    put(2 + j, part, block.T)

                @pl.when(core == 1)
                def _():
                    put(2 + part, j, block)
                    put(j, 2 + part, block.T)

        mine = pl.ds(pl.multiple_of(core * mid, mid), mid)
        theirs = pl.ds(pl.multiple_of(rows + core * mid, mid), mid)
        own = jnp.concatenate([excess[mine, :], excess[theirs, :]], axis=0)
        twice = jnp.dot(own, excess[...], preferred_element_type=jnp.float32)
        change = 0.375 * twice - 0.5 * own.astype(jnp.float32)
        row = lax.broadcasted_iota(jnp.int32, (rows, 2 * rows), 0)
        column = lax.broadcasted_iota(jnp.int32, (rows, 2 * rows), 1)
        diagonal = column == row + core * mid + jnp.where(row < mid, 0, rows - mid)
        weight = 1.0 + jnp.sum(jnp.where(diagonal, change, 0.0), axis=1, keepdims=True)
        change = jnp.where(diagonal, 0.0, change).astype(jnp.bfloat16)
        out = jnp.concatenate([x_ref[mine, :], y_ref[mine, :]], axis=0).astype(jnp.float32) * weight
        out += jnp.dot(change[:, 0:rows], x_ref[...], preferred_element_type=jnp.float32)
        out += jnp.dot(change[:, rows:2 * rows], y_ref[...], preferred_element_type=jnp.float32)
        near, far = out[0:mid], out[mid:rows]
        upper_half = jnp.where(core == 0, near, far).reshape(mid // tall, tall, width)
        lower_half = jnp.where(core == 0, far, near).reshape(mid // tall, tall, width)
        out = jnp.concatenate([upper_half, lower_half], axis=1).reshape(rows, width)
        out_ref[...] = out.astype(jnp.bfloat16)

    return pl.pallas_call(
        body,
        out_shape=jax.ShapeDtypeStruct((rows, width), jnp.bfloat16),
        scratch_shapes=[
            pltpu.VMEM((2 * stacked, BLOCK), jnp.float32),
            pltpu.VMEM((2 * rows, 2 * rows), jnp.bfloat16),
        ],
        compiler_params=VMEM_LIMIT,
    )


def full_rows(functions, pattern):
    bands, domains = lax.axis_size("band"), lax.axis_size("domain")
    devices, levels = bands * domains, domains // 2
    chips = devices // 2
    fdev, ncoef = functions.shape
    tall, width = fdev // 2, ncoef // chips
    rows = devices * tall
    spread = [[2 * q + c for q in chip_order(bands, levels)] for c in range(2)]
    order = [spread[0] + spread[1]]
    cut = functions.reshape(2, tall, chips, width).transpose(0, 2, 1, 3).reshape(devices, tall, width)
    x = lax.all_to_all(cut, BOTH, split_axis=0, concat_axis=0, axis_index_groups=order).reshape(rows, width)
    y = swap(x, "domain", 1)
    own = own_gram(width, NC // chips, bands)(x)
    pieces = cross_gram(width, bands)(x, y, own)
    total = pieces[0]
    for m in range(1, bands):
        total = total + swap(pieces[m], "band", m)
    heard = [total] + [swap(total, "domain", 2 * m) for m in range(1, levels)]
    while len(heard) > 1:
        heard = [heard[k] + heard[k + 1] for k in range(0, len(heard), 2)]
    excess = (heard[0] * (1.0 / NC)).astype(jnp.bfloat16)
    mine = [excess] + [swap(excess, "band", m) for m in range(1, bands)]
    other = [swap(e, "domain", 1) for e in mine]
    out = correct(width, bands, tall)(x, y, *mine, *other).reshape(chips, fdev, width)
    back = lax.all_to_all(out, BOTH, split_axis=0, concat_axis=0, axis_index_groups=spread)
    return back.transpose(1, 0, 2).reshape(fdev, ncoef)


def apply_blocks(excess, block_index, source_blocks):
    picked = jnp.take(source_blocks, block_index, axis=0)
    return jnp.einsum("bkij,bkjc->bic", excess, picked, preferred_element_type=jnp.float32)


def some_rows(functions, pattern):
    domains = lax.axis_size("domain")
    fdev = functions.shape[0]
    my_band = lax.axis_index("band")
    group = domains * fdev
    pieces = lax.all_to_all(functions, "domain", split_axis=1, concat_axis=0, tiled=True)
    every = lax.all_gather(pieces, "band", axis=0, tiled=True)
    width = every.shape[1]
    nblocks = every.shape[0] // BLOCK
    blocks = every.reshape(nblocks, BLOCK, width)
    rowblk = group // BLOCK
    block_index = lax.dynamic_slice_in_dim(pattern, my_band * rowblk, rowblk, 0)
    own_rows = pieces.reshape(rowblk, BLOCK, width)
    partners = jnp.take(blocks, block_index, axis=0)
    partial_sums = jnp.einsum(
        "bic,bkjc->bkij", own_rows, partners, preferred_element_type=jnp.float32
    )
    block_ids = my_band * rowblk + jnp.arange(rowblk, dtype=jnp.int32)
    on_diagonal = (block_index == block_ids[:, None]).astype(jnp.float32)
    total = lax.psum(partial_sums, "domain") * (1.0 / NC)
    identity = jnp.eye(BLOCK, dtype=jnp.float32)
    excess = (total - on_diagonal[:, :, None, None] * identity).astype(jnp.bfloat16)
    first = apply_blocks(excess, block_index, blocks)
    first_half = first.astype(jnp.bfloat16).reshape(group, width)
    all_first = lax.all_gather(first_half, "band", axis=0, tiled=True)
    first_blocks = all_first.reshape(nblocks, BLOCK, width)
    second = apply_blocks(excess, block_index, first_blocks)
    updated = own_rows.astype(jnp.float32) - 0.5 * first + 0.375 * second
    updated = updated.astype(jnp.bfloat16).reshape(group, width)
    return lax.all_to_all(updated, "domain", split_axis=0, concat_axis=1, tiled=True)


def per_device(functions, pattern):
    nblocks, nonzero = pattern.shape
    return (full_rows if nonzero == nblocks == 4 else some_rows)(functions, pattern)


def solution(mesh):
    placed = (P(BOTH, None), P())
    return jax.shard_map(
        per_device,
        mesh=mesh,
        in_specs=placed,
        out_specs=P(BOTH, None),
        check_vma=False,
    )
```

```python
import functools

import jax
import jax.numpy as jnp
from jax import lax
from jax.experimental import pallas as pl
from jax.experimental.pallas import tpu as pltpu
from jax.sharding import PartitionSpec as P

NC = 24576
BLOCK = 128
BOTH = ("band", "domain")
MEASURED = (10, 14, 12, 1, 9, 0, 3, 8, 2, 11, 7, 4, 13, 6, 15, 5)


VMEM_LIMIT = pltpu.CompilerParams(vmem_limit_bytes=16 * 1024 * 1024)


def my_core():
    return lax.rem(lax.axis_index("domain"), 2)


def swap(value, axis, mask):
    count = lax.axis_size(axis)
    return lax.ppermute(value, axis, [(i, i ^ mask) for i in range(count)])


ACROSS = (((1,), (1,)), ((), ()))


def chip_order(bands, levels):
    if (bands, levels) == (4, 4):
        return MEASURED
    return sorted(range(bands * levels), key=lambda q: (q // levels, abs(q % levels - levels // 2), q))


def squares():
    shape = (BLOCK, BLOCK)
    return lax.broadcasted_iota(jnp.int32, shape, 0), lax.broadcasted_iota(jnp.int32, shape, 1)


def heights(bands):
    body = 4 * BLOCK
    piece = -(-(body + 8) // (8 * bands)) * 8
    return body, piece * bands - body, piece


def own_gram(width, share, bands):
    _, tail, _ = heights(bands)

    def body(x_ref, out_ref):
        row, column = squares()
        got = lax.dot_general(x_ref[...], x_ref[...], ACROSS, preferred_element_type=jnp.float32)
        eye = jnp.where(row == column, share, 0.0).astype(jnp.float32)
        first, second = got[0:BLOCK, 0:BLOCK] - eye, got[BLOCK:, BLOCK:] - eye
        out_ref[0:BLOCK, :] = jnp.where(row <= column, first, second)
        out_ref[BLOCK:2 * BLOCK, :] = got[0:BLOCK, BLOCK:]
        line = jnp.sum(jnp.where(row == column, second, 0.0), axis=0, keepdims=True)
        out_ref[2 * BLOCK:2 * BLOCK + tail, :] = jnp.broadcast_to(line, (tail, BLOCK))

    return pl.pallas_call(
        body,
        out_shape=jax.ShapeDtypeStruct((2 * BLOCK + tail, BLOCK), jnp.float32),
        compiler_params=VMEM_LIMIT,
        cost_estimate=pl.CostEstimate(
            flops=8 * BLOCK * BLOCK * width, bytes_accessed=4 * BLOCK * width, transcendentals=0
        ),
    )


def cross_gram(width, bands):
    whole, tail, piece = heights(bands)

    def body(x_ref, y_ref, own_ref, *refs):
        piece_refs, stack = refs[:-1], refs[-1]
        core, band = my_core(), lax.axis_index("band")
        stack[0:2 * BLOCK, :] = own_ref[0:2 * BLOCK, :]
        stack[whole:whole + tail, :] = own_ref[2 * BLOCK:2 * BLOCK + tail, :]

        def put(left, right):
            got = lax.dot_general(left, right, ACROSS, preferred_element_type=jnp.float32)
            for j in range(2):
                stack[(2 + j) * BLOCK:(3 + j) * BLOCK, :] = got[:, j * BLOCK:(j + 1) * BLOCK]

        @pl.when(core == 0)
        def _():
            put(x_ref[0:BLOCK, :], y_ref[...])

        @pl.when(core == 1)
        def _():
            put(y_ref[BLOCK:2 * BLOCK, :], x_ref[...])

        for m in range(bands):
            at = pl.ds(pl.multiple_of((band ^ m) * piece, 8), piece)
            piece_refs[m][...] = stack[at, :]

    return pl.pallas_call(
        body,
        out_shape=tuple(jax.ShapeDtypeStruct((piece, BLOCK), jnp.float32) for _ in range(bands)),
        scratch_shapes=[pltpu.VMEM((whole + tail, BLOCK), jnp.float32)],
        compiler_params=VMEM_LIMIT,
        cost_estimate=pl.CostEstimate(
            flops=4 * BLOCK * BLOCK * width, bytes_accessed=8 * BLOCK * width, transcendentals=0
        ),
    )


def correct(width, bands):
    whole, tail, piece = heights(bands)
    stacked = whole + tail
    rows = 2 * BLOCK

    def body(x_ref, y_ref, *refs):
        piece_refs, out_ref, packed, excess = refs[:-3], refs[-3], refs[-2], refs[-1]
        band, core = lax.axis_index("band"), my_core()
        for side in range(2):
            for m in range(bands):
                start = side * stacked + (band ^ m) * piece
                held = piece_refs[side * bands + m][...].astype(jnp.float32)
                packed[pl.ds(pl.multiple_of(start, 8), piece), :] = held

        def put(row, column, block):
            at = (slice(row * BLOCK, (row + 1) * BLOCK), slice(column * BLOCK, (column + 1) * BLOCK))
            excess[at] = block.astype(jnp.bfloat16)

        row, column = squares()
        for side in range(2):
            at = side * stacked
            both, beside = packed[at:at + BLOCK, :], packed[at + BLOCK:at + 2 * BLOCK, :]
            line = packed[at + whole:at + whole + 8, :][0:1, :]
            turned = both.T
            put(2 * side, 2 * side, jnp.where(row <= column, both, turned))
            second = jnp.where(row > column, both, turned)
            put(2 * side + 1, 2 * side + 1, jnp.where(row == column, line, second))
            put(2 * side, 2 * side + 1, beside)
            put(2 * side + 1, 2 * side, beside.T)
        for part in range(2):
            for j in range(2):
                start = (part ^ core) * stacked + (2 + j) * BLOCK
                block = packed[pl.ds(pl.multiple_of(start, 8), BLOCK), :]

                @pl.when(core == 0)
                def _():
                    put(part, 2 + j, block)
                    put(2 + j, part, block.T)

                @pl.when(core == 1)
                def _():
                    put(2 + part, j, block)
                    put(j, 2 + part, block.T)

        own = excess[0:rows, :]
        twice = jnp.dot(own, excess[...], preferred_element_type=jnp.float32)
        change = 0.375 * twice - 0.5 * own.astype(jnp.float32)
        place = (rows, 2 * rows)
        diagonal = lax.broadcasted_iota(jnp.int32, place, 0) == lax.broadcasted_iota(jnp.int32, place, 1)
        weight = 1.0 + jnp.sum(jnp.where(diagonal, change, 0.0), axis=1, keepdims=True)
        change = jnp.where(diagonal, 0.0, change).astype(jnp.bfloat16)
        out = x_ref[...].astype(jnp.float32) * weight
        out += jnp.dot(change[:, 0:rows], x_ref[...], preferred_element_type=jnp.float32)
        out += jnp.dot(change[:, rows:2 * rows], y_ref[...], preferred_element_type=jnp.float32)
        out_ref[...] = out.astype(jnp.bfloat16)

    return pl.pallas_call(
        body,
        out_shape=jax.ShapeDtypeStruct((rows, width), jnp.bfloat16),
        scratch_shapes=[
            pltpu.VMEM((2 * stacked, BLOCK), jnp.float32),
            pltpu.VMEM((2 * rows, 2 * rows), jnp.bfloat16),
        ],
        compiler_params=VMEM_LIMIT,
    )


def full_rows(functions, pattern):
    bands, domains = lax.axis_size("band"), lax.axis_size("domain")
    devices, levels = bands * domains, domains // 2
    chips = devices // 2
    fdev, ncoef = functions.shape
    width, rows = ncoef // chips, chips * fdev
    spread = [[2 * q + c for q in chip_order(bands, levels)] for c in range(2)]
    cut = functions.reshape(fdev, chips, width).transpose(1, 0, 2)
    x = lax.all_to_all(cut, BOTH, split_axis=0, concat_axis=0, axis_index_groups=spread).reshape(rows, width)
    y = swap(x, "domain", 1)
    own = own_gram(width, NC // chips, bands)(x)
    pieces = cross_gram(width, bands)(x, y, own)
    total = pieces[0]
    for m in range(1, bands):
        total = total + swap(pieces[m], "band", m)
    heard = [total] + [swap(total, "domain", 2 * m) for m in range(1, levels)]
    while len(heard) > 1:
        heard = [heard[k] + heard[k + 1] for k in range(0, len(heard), 2)]
    excess = (heard[0] * (1.0 / NC)).astype(jnp.bfloat16)
    mine = [excess] + [swap(excess, "band", m) for m in range(1, bands)]
    other = [swap(e, "domain", 1) for e in mine]
    out = correct(width, bands)(x, y, *mine, *other).reshape(chips, fdev, width)
    back = lax.all_to_all(out, BOTH, split_axis=0, concat_axis=0, axis_index_groups=spread)
    return back.transpose(1, 0, 2).reshape(fdev, ncoef)


def apply_blocks(excess, block_index, source_blocks):
    picked = jnp.take(source_blocks, block_index, axis=0)
    return jnp.einsum("bkij,bkjc->bic", excess, picked, preferred_element_type=jnp.float32)


def some_rows(functions, pattern):
    domains = lax.axis_size("domain")
    fdev = functions.shape[0]
    my_band = lax.axis_index("band")
    group = domains * fdev
    pieces = lax.all_to_all(functions, "domain", split_axis=1, concat_axis=0, tiled=True)
    every = lax.all_gather(pieces, "band", axis=0, tiled=True)
    width = every.shape[1]
    nblocks = every.shape[0] // BLOCK
    blocks = every.reshape(nblocks, BLOCK, width)
    rowblk = group // BLOCK
    block_index = lax.dynamic_slice_in_dim(pattern, my_band * rowblk, rowblk, 0)
    own_rows = pieces.reshape(rowblk, BLOCK, width)
    partners = jnp.take(blocks, block_index, axis=0)
    partial_sums = jnp.einsum(
        "bic,bkjc->bkij", own_rows, partners, preferred_element_type=jnp.float32
    )
    block_ids = my_band * rowblk + jnp.arange(rowblk, dtype=jnp.int32)
    on_diagonal = (block_index == block_ids[:, None]).astype(jnp.float32)
    total = lax.psum(partial_sums, "domain") * (1.0 / NC)
    identity = jnp.eye(BLOCK, dtype=jnp.float32)
    excess = (total - on_diagonal[:, :, None, None] * identity).astype(jnp.bfloat16)
    first = apply_blocks(excess, block_index, blocks)
    first_half = first.astype(jnp.bfloat16).reshape(group, width)
    all_first = lax.all_gather(first_half, "band", axis=0, tiled=True)
    first_blocks = all_first.reshape(nblocks, BLOCK, width)
    second = apply_blocks(excess, block_index, first_blocks)
    updated = own_rows.astype(jnp.float32) - 0.5 * first + 0.375 * second
    updated = updated.astype(jnp.bfloat16).reshape(group, width)
    return lax.all_to_all(updated, "domain", split_axis=0, concat_axis=1, tiled=True)


def per_device(functions, pattern):
    nblocks, nonzero = pattern.shape
    return (full_rows if nonzero == nblocks == 4 else some_rows)(functions, pattern)


def solution(mesh):
    placed = (P(BOTH, None), P())
    return jax.shard_map(
        per_device,
        mesh=mesh,
        in_specs=placed,
        out_specs=P(BOTH, None),
        check_vma=False,
    )
```

```python
import functools

import jax
import jax.numpy as jnp
from jax import lax
from jax.experimental import pallas as pl
from jax.experimental.pallas import tpu as pltpu
from jax.sharding import PartitionSpec as P

NC = 24576
BLOCK = 128
BOTH = ("band", "domain")
MEASURED = (10, 14, 12, 1, 9, 0, 3, 8, 2, 11, 7, 4, 13, 6, 15, 5)


VMEM_LIMIT = pltpu.CompilerParams(vmem_limit_bytes=16 * 1024 * 1024)


def my_core():
    return lax.rem(lax.axis_index("domain"), 2)


def swap(value, axis, mask):
    count = lax.axis_size(axis)
    return lax.ppermute(value, axis, [(i, i ^ mask) for i in range(count)])


ACROSS = (((1,), (1,)), ((), ()))


def chip_order(bands, levels):
    if (bands, levels) == (4, 4):
        return MEASURED
    return sorted(range(bands * levels), key=lambda q: (q // levels, abs(q % levels - levels // 2), q))


def squares():
    shape = (BLOCK, BLOCK)
    return lax.broadcasted_iota(jnp.int32, shape, 0), lax.broadcasted_iota(jnp.int32, shape, 1)


def heights(bands):
    body = 4 * BLOCK
    piece = -(-(body + 8) // (8 * bands)) * 8
    return body, piece * bands - body, piece


def own_gram(width, share, bands):
    _, tail, _ = heights(bands)

    def body(x_ref, out_ref):
        row, column = squares()
        got = lax.dot_general(x_ref[...], x_ref[...], ACROSS, preferred_element_type=jnp.float32)
        eye = jnp.where(row == column, share, 0.0).astype(jnp.float32)
        first, second = got[0:BLOCK, 0:BLOCK] - eye, got[BLOCK:, BLOCK:] - eye
        out_ref[0:BLOCK, :] = jnp.where(row <= column, first, second)
        out_ref[BLOCK:2 * BLOCK, :] = got[0:BLOCK, BLOCK:]
        line = jnp.sum(jnp.where(row == column, second, 0.0), axis=0, keepdims=True)
        out_ref[2 * BLOCK:2 * BLOCK + tail, :] = jnp.broadcast_to(line, (tail, BLOCK))

    return pl.pallas_call(
        body,
        out_shape=jax.ShapeDtypeStruct((2 * BLOCK + tail, BLOCK), jnp.float32),
        compiler_params=VMEM_LIMIT,
        cost_estimate=pl.CostEstimate(
            flops=8 * BLOCK * BLOCK * width, bytes_accessed=4 * BLOCK * width, transcendentals=0
        ),
    )


def cross_gram(width, bands):
    whole, tail, piece = heights(bands)

    def body(x_ref, y_ref, own_ref, *refs):
        piece_refs, stack = refs[:-1], refs[-1]
        core, band = my_core(), lax.axis_index("band")
        stack[0:2 * BLOCK, :] = own_ref[0:2 * BLOCK, :]
        stack[whole:whole + tail, :] = own_ref[2 * BLOCK:2 * BLOCK + tail, :]

        def put(left, right):
            got = lax.dot_general(left, right, ACROSS, preferred_element_type=jnp.float32)
            for j in range(2):
                stack[(2 + j) * BLOCK:(3 + j) * BLOCK, :] = got[:, j * BLOCK:(j + 1) * BLOCK]

        @pl.when(core == 0)
        def _():
            put(x_ref[0:BLOCK, :], y_ref[...])

        @pl.when(core == 1)
        def _():
            put(y_ref[BLOCK:2 * BLOCK, :], x_ref[...])

        for m in range(bands):
            at = pl.ds(pl.multiple_of((band ^ m) * piece, 8), piece)
            piece_refs[m][...] = stack[at, :]

    return pl.pallas_call(
        body,
        out_shape=tuple(jax.ShapeDtypeStruct((piece, BLOCK), jnp.float32) for _ in range(bands)),
        scratch_shapes=[pltpu.VMEM((whole + tail, BLOCK), jnp.float32)],
        compiler_params=VMEM_LIMIT,
        cost_estimate=pl.CostEstimate(
            flops=4 * BLOCK * BLOCK * width, bytes_accessed=8 * BLOCK * width, transcendentals=0
        ),
    )


def unstack(piece_refs, packed, bands):
    whole, tail, piece = heights(bands)
    band = lax.axis_index("band")
    for m in range(bands):
        packed[pl.ds(pl.multiple_of((band ^ m) * piece, 8), piece), :] = piece_refs[m][...].astype(jnp.float32)
    row, column = squares()
    both, beside = packed[0:BLOCK, :], packed[BLOCK:2 * BLOCK, :]
    line = packed[whole:whole + 8, :][0:1, :]
    turned = both.T
    first = jnp.where(row <= column, both, turned)
    second = jnp.where(row == column, line, jnp.where(row > column, both, turned))
    grid = ((first, beside), (beside.T, second))
    return grid, [packed[(2 + j) * BLOCK:(3 + j) * BLOCK, :] for j in range(2)]


def block_at(row, column):
    return slice(row * BLOCK, (row + 1) * BLOCK), slice(column * BLOCK, (column + 1) * BLOCK)


def own_side(bands):
    whole, tail, _ = heights(bands)

    def body(*refs):
        piece_refs, square_ref, cross_ref, turned_ref, packed = refs[:-4], refs[-4], refs[-3], refs[-2], refs[-1]
        grid, cross = unstack(piece_refs, packed, bands)
        for i in range(2):
            for j in range(2):
                square_ref[block_at(i, j)] = grid[i][j].astype(jnp.bfloat16)
            cross_ref[block_at(0, i)] = cross[i].astype(jnp.bfloat16)
            turned_ref[block_at(i, 0)] = cross[i].T.astype(jnp.bfloat16)

    return pl.pallas_call(
        body,
        out_shape=(
            jax.ShapeDtypeStruct((2 * BLOCK, 2 * BLOCK), jnp.bfloat16),
            jax.ShapeDtypeStruct((BLOCK, 2 * BLOCK), jnp.bfloat16),
            jax.ShapeDtypeStruct((2 * BLOCK, BLOCK), jnp.bfloat16),
        ),
        scratch_shapes=[pltpu.VMEM((whole + tail, BLOCK), jnp.float32)],
        compiler_params=VMEM_LIMIT,
        cost_estimate=pl.CostEstimate(
            flops=16 * BLOCK * BLOCK, bytes_accessed=32 * BLOCK * BLOCK, transcendentals=0
        ),
    )


def correct(width, bands):
    whole, tail, _ = heights(bands)
    rows = 2 * BLOCK

    def body(x_ref, y_ref, square_ref, cross_ref, turned_ref, *refs):
        piece_refs, out_ref, packed, excess = refs[:-3], refs[-3], refs[-2], refs[-1]
        core = my_core()
        excess[0:rows, 0:rows] = square_ref[...]
        grid, cross = unstack(piece_refs, packed, bands)
        for i in range(2):
            for j in range(2):
                excess[block_at(2 + i, 2 + j)] = grid[i][j].astype(jnp.bfloat16)
        wide = jnp.concatenate(cross, axis=1).astype(jnp.bfloat16)
        tall = jnp.concatenate([c.T for c in cross], axis=0).astype(jnp.bfloat16)

        @pl.when(core == 0)
        def _():
            excess[0:BLOCK, rows:2 * rows] = cross_ref[...]
            excess[BLOCK:rows, rows:2 * rows] = wide
            excess[rows:2 * rows, 0:BLOCK] = turned_ref[...]
            excess[rows:2 * rows, BLOCK:rows] = tall

        @pl.when(core == 1)
        def _():
            excess[rows:rows + BLOCK, 0:rows] = wide
            excess[rows + BLOCK:2 * rows, 0:rows] = cross_ref[...]
            excess[0:rows, rows:rows + BLOCK] = tall
            excess[0:rows, rows + BLOCK:2 * rows] = turned_ref[...]

        own = excess[0:rows, :]
        twice = jnp.dot(own, excess[...], preferred_element_type=jnp.float32)
        change = 0.375 * twice - 0.5 * own.astype(jnp.float32)
        place = (rows, 2 * rows)
        diagonal = lax.broadcasted_iota(jnp.int32, place, 0) == lax.broadcasted_iota(jnp.int32, place, 1)
        weight = 1.0 + jnp.sum(jnp.where(diagonal, change, 0.0), axis=1, keepdims=True)
        change = jnp.where(diagonal, 0.0, change).astype(jnp.bfloat16)
        out = x_ref[...].astype(jnp.float32) * weight
        out += jnp.dot(change[:, 0:rows], x_ref[...], preferred_element_type=jnp.float32)
        out += jnp.dot(change[:, rows:2 * rows], y_ref[...], preferred_element_type=jnp.float32)
        out_ref[...] = out.astype(jnp.bfloat16)

    return pl.pallas_call(
        body,
        out_shape=jax.ShapeDtypeStruct((rows, width), jnp.bfloat16),
        scratch_shapes=[
            pltpu.VMEM((whole + tail, BLOCK), jnp.float32),
            pltpu.VMEM((2 * rows, 2 * rows), jnp.bfloat16),
        ],
        compiler_params=VMEM_LIMIT,
    )


def full_rows(functions, pattern):
    bands, domains = lax.axis_size("band"), lax.axis_size("domain")
    devices, levels = bands * domains, domains // 2
    chips = devices // 2
    fdev, ncoef = functions.shape
    width, rows = ncoef // chips, chips * fdev
    spread = [[2 * q + c for q in chip_order(bands, levels)] for c in range(2)]
    cut = functions.reshape(fdev, chips, width).transpose(1, 0, 2)
    x = lax.all_to_all(cut, BOTH, split_axis=0, concat_axis=0, axis_index_groups=spread).reshape(rows, width)
    y = swap(x, "domain", 1)
    own = own_gram(width, NC // chips, bands)(x)
    pieces = cross_gram(width, bands)(x, y, own)
    total = pieces[0]
    for m in range(1, bands):
        total = total + swap(pieces[m], "band", m)
    heard = [total] + [swap(total, "domain", 2 * m) for m in range(1, levels)]
    while len(heard) > 1:
        heard = [heard[k] + heard[k + 1] for k in range(0, len(heard), 2)]
    excess = (heard[0] * (1.0 / NC)).astype(jnp.bfloat16)
    mine = [excess] + [swap(excess, "band", m) for m in range(1, bands)]
    other = [swap(e, "domain", 1) for e in mine]
    out = correct(width, bands)(x, y, *own_side(bands)(*mine), *other).reshape(chips, fdev, width)
    back = lax.all_to_all(out, BOTH, split_axis=0, concat_axis=0, axis_index_groups=spread)
    return back.transpose(1, 0, 2).reshape(fdev, ncoef)


def apply_blocks(excess, block_index, source_blocks):
    picked = jnp.take(source_blocks, block_index, axis=0)
    return jnp.einsum("bkij,bkjc->bic", excess, picked, preferred_element_type=jnp.float32)


def some_rows(functions, pattern):
    domains = lax.axis_size("domain")
    fdev = functions.shape[0]
    my_band = lax.axis_index("band")
    group = domains * fdev
    pieces = lax.all_to_all(functions, "domain", split_axis=1, concat_axis=0, tiled=True)
    every = lax.all_gather(pieces, "band", axis=0, tiled=True)
    width = every.shape[1]
    nblocks = every.shape[0] // BLOCK
    blocks = every.reshape(nblocks, BLOCK, width)
    rowblk = group // BLOCK
    block_index = lax.dynamic_slice_in_dim(pattern, my_band * rowblk, rowblk, 0)
    own_rows = pieces.reshape(rowblk, BLOCK, width)
    partners = jnp.take(blocks, block_index, axis=0)
    partial_sums = jnp.einsum(
        "bic,bkjc->bkij", own_rows, partners, preferred_element_type=jnp.float32
    )
    block_ids = my_band * rowblk + jnp.arange(rowblk, dtype=jnp.int32)
    on_diagonal = (block_index == block_ids[:, None]).astype(jnp.float32)
    total = lax.psum(partial_sums, "domain") * (1.0 / NC)
    identity = jnp.eye(BLOCK, dtype=jnp.float32)
    excess = (total - on_diagonal[:, :, None, None] * identity).astype(jnp.bfloat16)
    first = apply_blocks(excess, block_index, blocks)
    first_half = first.astype(jnp.bfloat16).reshape(group, width)
    all_first = lax.all_gather(first_half, "band", axis=0, tiled=True)
    first_blocks = all_first.reshape(nblocks, BLOCK, width)
    second = apply_blocks(excess, block_index, first_blocks)
    updated = own_rows.astype(jnp.float32) - 0.5 * first + 0.375 * second
    updated = updated.astype(jnp.bfloat16).reshape(group, width)
    return lax.all_to_all(updated, "domain", split_axis=0, concat_axis=1, tiled=True)


def per_device(functions, pattern):
    nblocks, nonzero = pattern.shape
    return (full_rows if nonzero == nblocks == 4 else some_rows)(functions, pattern)


def solution(mesh):
    placed = (P(BOTH, None), P())
    return jax.shard_map(
        per_device,
        mesh=mesh,
        in_specs=placed,
        out_specs=P(BOTH, None),
        check_vma=False,
    )
```

```python
import functools

import jax
import jax.numpy as jnp
from jax import lax
from jax.experimental import pallas as pl
from jax.experimental.pallas import tpu as pltpu
from jax.sharding import PartitionSpec as P

NC = 24576
BLOCK = 128
BOTH = ("band", "domain")
MEASURED = (14, 10, 8, 5, 13, 4, 7, 12, 6, 15, 3, 0, 9, 2, 11, 1)


VMEM_LIMIT = pltpu.CompilerParams(vmem_limit_bytes=16 * 1024 * 1024)


def my_core():
    return lax.rem(lax.axis_index("domain"), 2)


def swap(value, axis, mask):
    count = lax.axis_size(axis)
    return lax.ppermute(value, axis, [(i, i ^ mask) for i in range(count)])


ACROSS = (((1,), (1,)), ((), ()))


def chip_order(bands, levels):
    if (bands, levels) == (4, 4):
        return MEASURED
    return sorted(range(bands * levels), key=lambda q: (q // levels, abs(q % levels - levels // 2), q))


def squares():
    shape = (BLOCK, BLOCK)
    return lax.broadcasted_iota(jnp.int32, shape, 0), lax.broadcasted_iota(jnp.int32, shape, 1)


def heights(bands):
    body = 4 * BLOCK
    piece = -(-(body + 8) // (8 * bands)) * 8
    return body, piece * bands - body, piece


def own_gram(width, share, bands):
    _, tail, _ = heights(bands)

    def body(x_ref, out_ref):
        row, column = squares()
        got = lax.dot_general(x_ref[...], x_ref[...], ACROSS, preferred_element_type=jnp.float32)
        eye = jnp.where(row == column, share, 0.0).astype(jnp.float32)
        first, second = got[0:BLOCK, 0:BLOCK] - eye, got[BLOCK:, BLOCK:] - eye
        out_ref[0:BLOCK, :] = jnp.where(row <= column, first, second)
        out_ref[BLOCK:2 * BLOCK, :] = got[0:BLOCK, BLOCK:]
        line = jnp.sum(jnp.where(row == column, second, 0.0), axis=0, keepdims=True)
        out_ref[2 * BLOCK:2 * BLOCK + tail, :] = jnp.broadcast_to(line, (tail, BLOCK))

    return pl.pallas_call(
        body,
        out_shape=jax.ShapeDtypeStruct((2 * BLOCK + tail, BLOCK), jnp.float32),
        compiler_params=VMEM_LIMIT,
        cost_estimate=pl.CostEstimate(
            flops=8 * BLOCK * BLOCK * width, bytes_accessed=4 * BLOCK * width, transcendentals=0
        ),
    )


def cross_gram(width, bands):
    whole, tail, piece = heights(bands)

    def body(x_ref, y_ref, own_ref, *refs):
        piece_refs, stack = refs[:-1], refs[-1]
        core, band = my_core(), lax.axis_index("band")
        stack[0:2 * BLOCK, :] = own_ref[0:2 * BLOCK, :]
        stack[whole:whole + tail, :] = own_ref[2 * BLOCK:2 * BLOCK + tail, :]

        def put(left, right):
            got = lax.dot_general(left, right, ACROSS, preferred_element_type=jnp.float32)
            for j in range(2):
                stack[(2 + j) * BLOCK:(3 + j) * BLOCK, :] = got[:, j * BLOCK:(j + 1) * BLOCK]

        @pl.when(core == 0)
        def _():
            put(x_ref[0:BLOCK, :], y_ref[...])

        @pl.when(core == 1)
        def _():
            put(y_ref[BLOCK:2 * BLOCK, :], x_ref[...])

        for m in range(bands):
            at = pl.ds(pl.multiple_of((band ^ m) * piece, 8), piece)
            piece_refs[m][...] = stack[at, :]

    return pl.pallas_call(
        body,
        out_shape=tuple(jax.ShapeDtypeStruct((piece, BLOCK), jnp.float32) for _ in range(bands)),
        scratch_shapes=[pltpu.VMEM((whole + tail, BLOCK), jnp.float32)],
        compiler_params=VMEM_LIMIT,
        cost_estimate=pl.CostEstimate(
            flops=4 * BLOCK * BLOCK * width, bytes_accessed=8 * BLOCK * width, transcendentals=0
        ),
    )


def unstack(piece_refs, packed, bands):
    whole, tail, piece = heights(bands)
    band = lax.axis_index("band")
    for m in range(bands):
        packed[pl.ds(pl.multiple_of((band ^ m) * piece, 8), piece), :] = piece_refs[m][...].astype(jnp.float32)
    row, column = squares()
    both, beside = packed[0:BLOCK, :], packed[BLOCK:2 * BLOCK, :]
    line = packed[whole:whole + 8, :][0:1, :]
    turned = both.T
    first = jnp.where(row <= column, both, turned)
    second = jnp.where(row == column, line, jnp.where(row > column, both, turned))
    grid = ((first, beside), (beside.T, second))
    return grid, [packed[(2 + j) * BLOCK:(3 + j) * BLOCK, :] for j in range(2)]


def block_at(row, column):
    return slice(row * BLOCK, (row + 1) * BLOCK), slice(column * BLOCK, (column + 1) * BLOCK)


def own_side(bands):
    whole, tail, _ = heights(bands)

    def body(*refs):
        piece_refs, square_ref, cross_ref, turned_ref, packed = refs[:-4], refs[-4], refs[-3], refs[-2], refs[-1]
        grid, cross = unstack(piece_refs, packed, bands)
        for i in range(2):
            for j in range(2):
                square_ref[block_at(i, j)] = grid[i][j].astype(jnp.bfloat16)
            cross_ref[block_at(0, i)] = cross[i].astype(jnp.bfloat16)
            turned_ref[block_at(i, 0)] = cross[i].T.astype(jnp.bfloat16)

    return pl.pallas_call(
        body,
        out_shape=(
            jax.ShapeDtypeStruct((2 * BLOCK, 2 * BLOCK), jnp.bfloat16),
            jax.ShapeDtypeStruct((BLOCK, 2 * BLOCK), jnp.bfloat16),
            jax.ShapeDtypeStruct((2 * BLOCK, BLOCK), jnp.bfloat16),
        ),
        scratch_shapes=[pltpu.VMEM((whole + tail, BLOCK), jnp.float32)],
        compiler_params=VMEM_LIMIT,
        cost_estimate=pl.CostEstimate(
            flops=16 * BLOCK * BLOCK, bytes_accessed=32 * BLOCK * BLOCK, transcendentals=0
        ),
    )


def correct(width, bands):
    whole, tail, _ = heights(bands)
    rows = 2 * BLOCK

    def body(x_ref, y_ref, square_ref, cross_ref, turned_ref, *refs):
        piece_refs, out_ref, packed, excess = refs[:-3], refs[-3], refs[-2], refs[-1]
        core = my_core()
        excess[0:rows, 0:rows] = square_ref[...]
        grid, cross = unstack(piece_refs, packed, bands)
        for i in range(2):
            for j in range(2):
                excess[block_at(2 + i, 2 + j)] = grid[i][j].astype(jnp.bfloat16)
        wide = jnp.concatenate(cross, axis=1).astype(jnp.bfloat16)
        tall = jnp.concatenate([c.T for c in cross], axis=0).astype(jnp.bfloat16)

        @pl.when(core == 0)
        def _():
            excess[0:BLOCK, rows:2 * rows] = cross_ref[...]
            excess[BLOCK:rows, rows:2 * rows] = wide
            excess[rows:2 * rows, 0:BLOCK] = turned_ref[...]
            excess[rows:2 * rows, BLOCK:rows] = tall

        @pl.when(core == 1)
        def _():
            excess[rows:rows + BLOCK, 0:rows] = wide
            excess[rows + BLOCK:2 * rows, 0:rows] = cross_ref[...]
            excess[0:rows, rows:rows + BLOCK] = tall
            excess[0:rows, rows + BLOCK:2 * rows] = turned_ref[...]

        own = excess[0:rows, :]
        twice = jnp.dot(own, excess[...], preferred_element_type=jnp.float32)
        change = 0.375 * twice - 0.5 * own.astype(jnp.float32)
        place = (rows, 2 * rows)
        diagonal = lax.broadcasted_iota(jnp.int32, place, 0) == lax.broadcasted_iota(jnp.int32, place, 1)
        weight = 1.0 + jnp.sum(jnp.where(diagonal, change, 0.0), axis=1, keepdims=True)
        change = jnp.where(diagonal, 0.0, change).astype(jnp.bfloat16)
        out = x_ref[...].astype(jnp.float32) * weight
        out += jnp.dot(change[:, 0:rows], x_ref[...], preferred_element_type=jnp.float32)
        out += jnp.dot(change[:, rows:2 * rows], y_ref[...], preferred_element_type=jnp.float32)
        out_ref[...] = out.astype(jnp.bfloat16)

    return pl.pallas_call(
        body,
        out_shape=jax.ShapeDtypeStruct((rows, width), jnp.bfloat16),
        scratch_shapes=[
            pltpu.VMEM((whole + tail, BLOCK), jnp.float32),
            pltpu.VMEM((2 * rows, 2 * rows), jnp.bfloat16),
        ],
        compiler_params=VMEM_LIMIT,
    )


def full_rows(functions, pattern):
    bands, domains = lax.axis_size("band"), lax.axis_size("domain")
    devices, levels = bands * domains, domains // 2
    chips = devices // 2
    fdev, ncoef = functions.shape
    width, rows = ncoef // chips, chips * fdev
    spread = [[2 * q + c for q in chip_order(bands, levels)] for c in range(2)]
    cut = functions.reshape(fdev, chips, width).transpose(1, 0, 2)
    x = lax.all_to_all(cut, BOTH, split_axis=0, concat_axis=0, axis_index_groups=spread).reshape(rows, width)
    y = swap(x, "domain", 1)
    own = own_gram(width, NC // chips, bands)(x)
    pieces = cross_gram(width, bands)(x, y, own)
    total = pieces[0]
    for m in range(1, bands):
        total = total + swap(pieces[m], "band", m)
    heard = [total] + [swap(total, "domain", 2 * m) for m in range(1, levels)]
    while len(heard) > 1:
        heard = [heard[k] + heard[k + 1] for k in range(0, len(heard), 2)]
    excess = (heard[0] * (1.0 / NC)).astype(jnp.bfloat16)
    mine = [excess] + [swap(excess, "band", m) for m in range(1, bands)]
    other = [swap(e, "domain", 1) for e in mine]
    out = correct(width, bands)(x, y, *own_side(bands)(*mine), *other).reshape(chips, fdev, width)
    back = lax.all_to_all(out, BOTH, split_axis=0, concat_axis=0, axis_index_groups=spread)
    return back.transpose(1, 0, 2).reshape(fdev, ncoef)


def apply_blocks(excess, block_index, source_blocks):
    picked = jnp.take(source_blocks, block_index, axis=0)
    return jnp.einsum("bkij,bkjc->bic", excess, picked, preferred_element_type=jnp.float32)


def some_rows(functions, pattern):
    domains = lax.axis_size("domain")
    fdev = functions.shape[0]
    my_band = lax.axis_index("band")
    group = domains * fdev
    pieces = lax.all_to_all(functions, "domain", split_axis=1, concat_axis=0, tiled=True)
    every = lax.all_gather(pieces, "band", axis=0, tiled=True)
    width = every.shape[1]
    nblocks = every.shape[0] // BLOCK
    blocks = every.reshape(nblocks, BLOCK, width)
    rowblk = group // BLOCK
    block_index = lax.dynamic_slice_in_dim(pattern, my_band * rowblk, rowblk, 0)
    own_rows = pieces.reshape(rowblk, BLOCK, width)
    partners = jnp.take(blocks, block_index, axis=0)
    partial_sums = jnp.einsum(
        "bic,bkjc->bkij", own_rows, partners, preferred_element_type=jnp.float32
    )
    block_ids = my_band * rowblk + jnp.arange(rowblk, dtype=jnp.int32)
    on_diagonal = (block_index == block_ids[:, None]).astype(jnp.float32)
    total = lax.psum(partial_sums, "domain") * (1.0 / NC)
    identity = jnp.eye(BLOCK, dtype=jnp.float32)
    excess = (total - on_diagonal[:, :, None, None] * identity).astype(jnp.bfloat16)
    first = apply_blocks(excess, block_index, blocks)
    first_half = first.astype(jnp.bfloat16).reshape(group, width)
    all_first = lax.all_gather(first_half, "band", axis=0, tiled=True)
    first_blocks = all_first.reshape(nblocks, BLOCK, width)
    second = apply_blocks(excess, block_index, first_blocks)
    updated = own_rows.astype(jnp.float32) - 0.5 * first + 0.375 * second
    updated = updated.astype(jnp.bfloat16).reshape(group, width)
    return lax.all_to_all(updated, "domain", split_axis=0, concat_axis=1, tiled=True)


def per_device(functions, pattern):
    nblocks, nonzero = pattern.shape
    return (full_rows if nonzero == nblocks == 4 else some_rows)(functions, pattern)


def solution(mesh):
    placed = (P(BOTH, None), P())
    return jax.shard_map(
        per_device,
        mesh=mesh,
        in_specs=placed,
        out_specs=P(BOTH, None),
        check_vma=False,
    )
```
